128 devices in a mesh: row: 16 (over z, x), col: 8 (over y, core).
Axes of the slice: x: 4, y: 4, z: 4, core: 2. Of those that a mesh axis runs over, the one named last changes fastest.
Arguments:
- block_pairs: int32 [128, 3, 2], P(('row', 'col')), may hold values from 0 to 127, as said below
- live_counts: int32 [128], P(('row', 'col')), may hold values from 1 to 3, as said below
- pair_blocks: bfloat16 [384, 1024, 1024], P(('row', 'col')), may hold values from -8 to 8, as said below
- start_basis: bfloat16 [128, 32, 1024], P(('row', 'col')), may hold values from -48 to 48
Outputs:
- first_basis: float32 [128, 32, 1024], P(('row', 'col'))
- embedding: float32 [128, 32, 1024], P(('row', 'col'))
The draws below stay inside these ranges and needn't reach their ends.
Inputs may be any that keep to these rules, and one draw needn't show every extreme that they name: `block_pairs`: slot s of device d = (row index) * 8 + (col index) holds (i, j) with i <= j, i // 8 equal to the row index and j % 8 equal to the col index; live slots of one device are distinct pairs, and no pair stands on two devices; slots beyond the live count repeat a live pair. `live_counts`: some device has 3 live slots. `pair_blocks`: the block of a slot with i = j is symmetric.
All inputs are finite; a program needn't handle non-finite values.
Results may differ from the reference program's by a relative error of at most 0.0021.
Values may be sent and summed in bfloat16 or wider, within the bound.
No kernel may reach another device: no remote copies, remote signals or barrier semaphores. Data moves between devices by JAX's collectives and lax.ppermute only.
A program may use at most 64 MiB of HBM per device.

```python
import math
import jax
import jax.numpy as jnp
from jax import lax

K = 32
BS = 1024
PAIRS_DEV = 3
NB = 128
USERS = 131072
N_ROW = 16
N_COL = 8
DEVICES = 128


def pair_layout(key):
    device = jnp.arange(DEVICES, dtype=jnp.int32)
    row_index = device // N_COL
    col_index = device % N_COL
    options = N_COL * (N_ROW - 1 - row_index) + col_index + 1
    first_key, second_key = jax.random.split(key)
    ceiling = jnp.minimum(options, PAIRS_DEV)
    alive = jax.random.randint(first_key, (DEVICES,), 0, 1 << 20) % ceiling + 1
    alive = alive.at[0].set(PAIRS_DEV)
    offsets = jax.random.randint(second_key, (DEVICES,), 0, 1 << 20) % options
    slot_ids = jnp.arange(PAIRS_DEV, dtype=jnp.int32)[None, :]
    picks = (offsets[:, None] + jnp.minimum(slot_ids, alive[:, None] - 1)) % options[:, None]
    beyond = picks - (col_index[:, None] + 1)
    inside = beyond < 0
    band_slot = jnp.where(inside, picks, beyond % N_COL)
    class_slot = jnp.where(inside, row_index[:, None], row_index[:, None] + 1 + beyond // N_COL)
    first = row_index[:, None] * N_COL + band_slot
    second = col_index[:, None] + N_COL * class_slot
    layout = jnp.stack([first, second], axis=-1).astype(jnp.int32)
    return (layout, alive.astype(jnp.int32))


def draw_block_pairs(key, part):
    layout, alive = pair_layout(key)
    return layout


def draw_live_counts(key, part):
    layout, alive = pair_layout(key)
    return alive


def draw_pair_blocks(key, part):
    layout, alive = pair_layout(key)
    key = jax.random.fold_in(key, 3)
    shape = (DEVICES * PAIRS_DEV, BS, BS)
    holder = (jnp.arange(DEVICES * PAIRS_DEV, dtype=jnp.int32) // PAIRS_DEV).astype(jnp.float32)
    fraction = holder / max(DEVICES - 1, 1)
    base = jnp.clip(jax.random.normal(key, shape, jnp.float32), -5.0, 5.0)
    rise = 1.0 + 2.0 * fraction
    flat = layout.reshape(-1, 2)
    same = (flat[:, 0] == flat[:, 1])[:, None, None]
    base = jnp.where(same, (base + jnp.swapaxes(base, 1, 2)) * 0.7071, base)
    return (base * rise[:, None, None] * BS ** (-0.5)).astype(jnp.bfloat16)


def draw_start_basis(key, part):
    key = jax.random.fold_in(key, 7)
    first_key, second_key = jax.random.split(key)
    shape = (DEVICES, K, BS)
    spread = jnp.exp(jax.random.uniform(second_key, (DEVICES, 1, BS), jnp.float32) * math.log(10.0)) / 3.0
    fraction = jnp.arange(DEVICES, dtype=jnp.float32) / max(DEVICES - 1, 1)
    base = jnp.clip(jax.random.normal(first_key, shape, jnp.float32), -4.0, 4.0)
    rise = 1.0 + 2.0 * fraction
    return (base * spread * rise[:, None, None]).astype(jnp.bfloat16)


def setup_inputs(seed: int = 0) -> dict:
    splits = jax.random.split(jax.random.key(seed), 5)
    block_pairs = draw_block_pairs(jax.random.fold_in(splits[4], 71), 0)
    live_counts = draw_live_counts(jax.random.fold_in(splits[4], 71), 0)
    pair_blocks = draw_pair_blocks(jax.random.fold_in(splits[4], 71), 0)
    start_basis = draw_start_basis(jax.random.fold_in(splits[4], 71), 0)
    return dict(block_pairs=block_pairs, live_counts=live_counts, pair_blocks=pair_blocks, start_basis=start_basis)


def multiply(block_pairs, live_counts, pair_blocks, panels):
    flat_pairs = block_pairs.reshape(-1, 2)
    slot_ids = jnp.arange(PAIRS_DEV, dtype=jnp.int32)[None, :]
    live_flags = (slot_ids < live_counts[:, None]).reshape(-1)

    def advance(totals, item):
        couple, alive, matrix = item
        first = couple[0]
        second = couple[1]
        left = lax.dynamic_index_in_dim(panels, second, 0, keepdims=False)
        right = lax.dynamic_index_in_dim(panels, first, 0, keepdims=False)
        direct = jnp.dot(left.astype(jnp.float32), matrix.T.astype(jnp.float32), preferred_element_type=jnp.float32)
        mirror = jnp.dot(right.astype(jnp.float32), matrix.astype(jnp.float32), preferred_element_type=jnp.float32)
        direct = jnp.where(alive, direct, 0.0)
        mirror = jnp.where(alive & (first != second), mirror, 0.0)
        totals = totals.at[first].add(direct)
        totals = totals.at[second].add(mirror)
        return (totals, None)
    totals = jnp.zeros((NB, K, BS), jnp.float32)
    totals, unused = lax.scan(advance, totals, (flat_pairs, live_flags, pair_blocks))
    return totals

def gram_matrix(values):
    values = values.astype(jnp.float32)
    return jnp.einsum('bkn,bln->kl', values, values, precision=lax.Precision.HIGHEST)

def lower_inverse(gram):
    factor = jnp.linalg.cholesky(gram)
    identity = jnp.eye(K, dtype=jnp.float32)
    return jax.scipy.linalg.solve_triangular(factor, identity, lower=True)

def reference(block_pairs, live_counts, pair_blocks, start_basis):
    first = multiply(block_pairs, live_counts, pair_blocks, start_basis)
    panels = first.astype(jnp.bfloat16)
    inverse_one = lower_inverse(gram_matrix(panels))
    first_basis = jnp.einsum('kl,bln->bkn', inverse_one, first, precision=lax.Precision.HIGHEST) * math.sqrt(USERS)
    second = multiply(block_pairs, live_counts, pair_blocks, panels)
    scaled = jnp.einsum('kl,bln->bkn', inverse_one, second, precision=lax.Precision.HIGHEST)
    inverse_two = lower_inverse(gram_matrix(scaled))
    result = jnp.einsum('kl,bln->bkn', inverse_two, scaled, precision=lax.Precision.HIGHEST)
    return (first_basis, result * math.sqrt(USERS))
```

```python
import functools

import jax
import jax.numpy as jnp
from jax import lax
from jax.experimental import pallas as pl
from jax.experimental.pallas import tpu as pltpu
from jax.sharding import PartitionSpec as P

BOTH = ("row", "col")
HIGHEST = lax.Precision.HIGHEST
VMEM = pl.BlockSpec(memory_space=pltpu.VMEM)
SMEM = pl.BlockSpec(memory_space=pltpu.SMEM)
ANY = pl.BlockSpec(memory_space=pl.ANY)
PARAMS = pltpu.CompilerParams(vmem_limit_bytes=48 * 1024 * 1024)


def permute(value, target):
    pairs = []
    for device in range(128):
        z, x, y, c = device // 32, device // 8 % 4, device // 2 % 4, device % 2
        tz, tx, ty, tc = target(z, x, y, c)
        pairs.append((device, ((tz % 4) * 4 + tx % 4) * 8 + (ty % 4) * 2 + tc % 2))
    return lax.ppermute(value, BOTH, pairs)


def send_inner(value, s):
    return permute(value, lambda z, x, y, c: (z + s, x, y, c) if c == 0 else (z, x + s, y, c))


def send_outer(value, s):
    return permute(value, lambda z, x, y, c: (z, x + s, y, c) if c == 0 else (z + s, x, y, c))


def send_y(value, s):
    return permute(value, lambda z, x, y, c: (z, x, y + s, c))


def send_z(value, s):
    return permute(value, lambda z, x, y, c: (z + s, x, y, c))


def send_x(value, s):
    return permute(value, lambda z, x, y, c: (z, x + s, y, c))


def send_core(value):
    return permute(value, lambda z, x, y, c: (z, x, y, c + 1))


def struct(shape, dtype):
    return jax.ShapeDtypeStruct(shape, dtype)


def product_kernel(pairs, live, blocks, g0, g1, g2, g3, h0, h1, *rest):
    gathered, pair_gathered = (g0, g1, g2, g3), (h0, h1)
    outs = rest[:6]
    matrices, lefts, rights, result, total, sems = rest[6:]
    count = live[0]
    row = pairs[0, 0, 0] // 8
    col = pairs[0, 0, 1] % 8
    z, x, y, c = row // 4, row % 4, col // 2, col % 2

    def shift(target):
        tz, tx = target // 4, target % 4
        dz, dx = (tz - z) & 3, (tx - x) & 3
        return jnp.where(c == 0, dx, dz), jnp.where(c == 0, dz, dx)

    def matrix_copy(slot):
        return pltpu.make_async_copy(blocks.at[slot], matrices.at[slot], sems.at[0, slot])

    def left_copy(slot, outer, inner):
        source = gathered[outer].at[inner, :, pl.ds(0, 1024)]
        return pltpu.make_async_copy(source, lefts.at[slot], sems.at[1, slot])

    def right_copy(slot, core, dy):
        source = pair_gathered[core].at[dy, :, pl.ds(0, 1024)]
        return pltpu.make_async_copy(source, rights.at[slot], sems.at[2, slot])

    for slot in range(3):
        @pl.when(slot < count)
        def _():
            matrix_copy(slot).start()

    for slot in range(3):
        @pl.when(slot < count)
        def _():
            first, second = pairs[0, slot, 0], pairs[0, slot, 1]
            outer, inner = shift(second // 8)
            outer, inner = (4 - outer) & 3, (4 - inner) & 3
            for t in range(4):
                @pl.when(outer == t)
                def _():
                    left_copy(slot, t, inner).start()
            dy = (y - first % 8 // 2) & 3
            dc = (first % 8 % 2) ^ c
            for t in range(2):
                @pl.when(dc == t)
                def _():
                    right_copy(slot, t, dy).start()

    total[...] = jnp.zeros_like(total)

    def advance(slot, carry):
        first, second = pairs[0, slot, 0], pairs[0, slot, 1]
        left_copy(slot, 0, 0).wait()
        right_copy(slot, 0, 0).wait()
        matrix_copy(slot).wait()
        outer, inner = shift(second // 8)
        dy = (first % 8 // 2 - y) & 3
        dc = (first % 8 % 2) ^ c
        band = 16 + dc * 4 + dy
        total[band] += lax.dot_general(
            lefts[slot], matrices[slot], (((1,), (1,)), ((), ())), preferred_element_type=jnp.float32
        )

        @pl.when(first != second)
        def _():
            part = outer * 4 + inner
            total[part] += lax.dot_general(
                rights[slot], matrices[slot], (((1,), (0,)), ((), ())), preferred_element_type=jnp.float32
            )

        return carry

    lax.fori_loop(0, count, advance, 0)
    for k, out in enumerate(outs):
        out[...] = total[4 * k : 4 * k + 4].astype(out.dtype)


def product(pairs, live, blocks, gathered, pair_gathered, sent):
    shape = (4, 32, 1024)
    f32 = jnp.float32
    return pl.pallas_call(
        product_kernel,
        out_shape=[struct(shape, f32)] + [struct(shape, sent)] * 3 + [struct(shape, f32), struct(shape, sent)],
        in_specs=[SMEM, SMEM] + [ANY] * 7,
        out_specs=[VMEM] * 6,
        scratch_shapes=[
            pltpu.VMEM((3, 1024, 1024), jnp.bfloat16),
            pltpu.VMEM((3, 32, 1024), jnp.bfloat16),
            pltpu.VMEM((3, 32, 1024), jnp.bfloat16),
            pltpu.VMEM((8, 128), f32),
            pltpu.VMEM((24, 32, 1024), f32),
            pltpu.SemaphoreType.DMA((3, 3)),
        ],
        compiler_params=PARAMS,
        cost_estimate=pl.CostEstimate(flops=800_000_000, bytes_accessed=10_000_000, transcendentals=0),
        name="product",
    )(pairs, live, blocks, *gathered, *pair_gathered)


def sum_kernel(own, *rest):
    received, outs = rest[: len(rest) - 4], rest[len(rest) - 4 :]
    for k, out in enumerate(outs):
        value = own[k]
        for array in received:
            value = value + array[k].astype(jnp.float32)
        out[...] = value.astype(out.dtype)


def add_received(own, received, sent):
    shape = (32, 1024)
    return pl.pallas_call(
        sum_kernel,
        out_shape=[struct(shape, jnp.float32)] + [struct(shape, sent)] * 3,
        in_specs=[VMEM] * (1 + len(received)),
        out_specs=[VMEM] * 4,
        compiler_params=PARAMS,
        name="add_received",
    )(own, *received)


def first_kernel(*refs):
    parts, (first, panel, gram) = refs[:8], refs[8:]
    value = parts[0][...] + parts[1][...]
    for part in parts[2:]:
        value = value + part[...].astype(jnp.float32)
    first[...] = value
    rounded = value.astype(jnp.bfloat16)
    panel[...] = rounded
    gram[...] = lax.dot_general(
        rounded, rounded, (((1,), (1,)), ((), ())), preferred_element_type=jnp.float32
    )


def finish_first(parts):
    return pl.pallas_call(
        first_kernel,
        out_shape=[
            struct((32, 1024), jnp.float32),
            struct((32, 1024), jnp.bfloat16),
            struct((32, 32), jnp.float32),
        ],
        in_specs=[VMEM] * 8,
        out_specs=[VMEM] * 3,
        compiler_params=PARAMS,
        name="finish_first",
    )(*parts)


def second_kernel(*refs):
    parts, inverse, (scaled, gram) = refs[:8], refs[8], refs[9:]
    value = parts[0][...] + parts[1][...]
    for part in parts[2:]:
        value = value + part[...].astype(jnp.float32)
    value = jnp.dot(inverse[...], value, precision=HIGHEST, preferred_element_type=jnp.float32)
    scaled[...] = value
    gram[...] = lax.dot_general(
        value, value, (((1,), (1,)), ((), ())), precision=HIGHEST, preferred_element_type=jnp.float32
    )


def finish_second(parts, inverse):
    return pl.pallas_call(
        second_kernel,
        out_shape=[struct((32, 1024), jnp.float32), struct((32, 32), jnp.float32)],
        in_specs=[VMEM] * 9,
        out_specs=[VMEM] * 2,
        compiler_params=PARAMS,
        name="finish_second",
    )(*parts, inverse)


def lower_inverse(gram):
    rows = lax.broadcasted_iota(jnp.int32, (32, 128), 0)
    lanes = lax.broadcasted_iota(jnp.int32, (32, 128), 1)
    wide = jnp.concatenate([gram, jnp.zeros((32, 96), jnp.float32)], axis=1)
    wide = jnp.where(lanes == rows + 32, 1.0, wide)
    for k in range(31):
        pivot = wide[k : k + 1, k : k + 1]
        factor = jnp.where(rows > k, wide[:, k : k + 1], 0.0)
        wide = wide - factor * (wide[k : k + 1, :] / pivot)
    diagonal = jnp.sum(jnp.where(lanes == rows, wide, 0.0), axis=1, keepdims=True)
    wide = wide / jnp.sqrt(diagonal)
    return wide[:, 32:64]


def factor_kernel(gram, panel, root, *outs):
    inverse = lower_inverse(gram[...])
    outs[0][...] = (
        jnp.dot(inverse, panel[...], precision=HIGHEST, preferred_element_type=jnp.float32) * root
    )
    if len(outs) > 1:
        outs[1][...] = inverse


def apply_factor(gram, panel, root, keep):
    return pl.pallas_call(
        lambda a, b, *outs: factor_kernel(a, b, root, *outs),
        out_shape=[struct((32, 1024), jnp.float32)] + [struct((32, 32), jnp.float32)] * keep,
        in_specs=[VMEM] * 2,
        out_specs=[VMEM] * (1 + keep),
        compiler_params=PARAMS,
        name="apply_factor",
    )(gram, panel)


SHIFTS = (1, 3, 2)


def spread(send, value):
    got = {s: send(value, s) for s in SHIFTS}
    return [value] + [got[s] for s in (1, 2, 3)]


def gather(panel):
    inner = jnp.stack(spread(send_inner, panel))
    along_y = jnp.stack(spread(send_y, panel))
    return spread(send_outer, inner), [along_y, send_core(along_y)]


def scatter(parts, sent):
    row_parts, pair_parts = parts[:4], parts[4:]
    got = {s: send_outer(row_parts[s], s) for s in SHIFTS}
    other = send_core(pair_parts[1])
    column = add_received(pair_parts[0], [other], sent)
    got_y = [send_y(column[s], s) for s in SHIFTS]
    row = add_received(row_parts[0], [got[s] for s in SHIFTS], sent)
    got_row = [send_inner(row[s], s) for s in SHIFTS]
    return [row[0], column[0]] + got_y + got_row


def total_gram(gram):
    gram = gram + send_core(gram)
    for send in (send_y, send_z, send_x):
        got = [send(gram, s) for s in SHIFTS]
        gram = gram + got[0] + got[1] + got[2]
    return gram


def on_device(block_pairs, live_counts, pair_blocks, start_basis):
    users = 128 * start_basis.shape[2]
    root = float(users) ** 0.5
    gathered, pair_gathered = gather(start_basis[0])
    parts = product(block_pairs, live_counts, pair_blocks, gathered, pair_gathered, jnp.float32)
    first, panel, gram = finish_first(scatter(parts, jnp.float32))
    gathered, pair_gathered = gather(panel)
    parts = product(block_pairs, live_counts, pair_blocks, gathered, pair_gathered, jnp.bfloat16)
    first_basis, inverse = apply_factor(total_gram(gram), first, root, 1)
    scaled, gram = finish_second(scatter(parts, jnp.bfloat16), inverse)
    (embedding,) = apply_factor(total_gram(gram), scaled, root, 0)
    return (first_basis[None], embedding[None])


def solution(mesh):
    spec = P(BOTH, None, None)
    return jax.shard_map(
        on_device, mesh=mesh, in_specs=(spec, P(BOTH), spec, spec), out_specs=(spec, spec), check_vma=False
    )
```

```python
import functools

import jax
import jax.numpy as jnp
from jax import lax
from jax.experimental import pallas as pl
from jax.experimental.pallas import tpu as pltpu
from jax.sharding import PartitionSpec as P

BOTH = ("row", "col")
HIGHEST = lax.Precision.HIGHEST
VMEM = pl.BlockSpec(memory_space=pltpu.VMEM)
SMEM = pl.BlockSpec(memory_space=pltpu.SMEM)
PARAMS = pltpu.CompilerParams(vmem_limit_bytes=24 * 1024 * 1024)


def permute(value, target):
    pairs = []
    for device in range(128):
        z, x, y, c = device // 32, device // 8 % 4, device // 2 % 4, device % 2
        tz, tx, ty, tc = target(z, x, y, c)
        pairs.append((device, ((tz % 4) * 4 + tx % 4) * 8 + (ty % 4) * 2 + tc % 2))
    return lax.ppermute(value, BOTH, pairs)


def send_inner(value, s):
    return permute(value, lambda z, x, y, c: (z + s, x, y, c) if c == 0 else (z, x + s, y, c))


def send_outer(value, s):
    return permute(value, lambda z, x, y, c: (z, x + s, y, c) if c == 0 else (z + s, x, y, c))


def send_y(value, s):
    return permute(value, lambda z, x, y, c: (z, x, y ^ s, c))


def send_core(value):
    return permute(value, lambda z, x, y, c: (z, x, y, c + 1))


def struct(shape, dtype):
    return jax.ShapeDtypeStruct(shape, dtype)


def fold(gram):
    return jnp.concatenate([gram[8 * k : 8 * k + 8] for k in range(4)], axis=1)


def unfold(tile):
    return jnp.concatenate([tile[:, 32 * k : 32 * k + 32] for k in range(4)], axis=0)


def split(tile):
    terms = []
    for _ in range(3):
        term = tile.astype(jnp.bfloat16).astype(jnp.float32)
        terms.append(term)
        tile = tile - term
    return jnp.concatenate(terms + [jnp.zeros_like(tile)], axis=0).astype(jnp.bfloat16)


def merge(terms):
    terms = terms.astype(jnp.float32)
    return terms[0:8] + terms[8:16] + terms[16:24]


def product_kernel(with_gram, pairs, live, blocks, g0, g1, g2, g3, h0, h1, *rest):
    gathered, pair_gathered = (g0, g1, g2, g3), (h0, h1)
    outs = rest[:6]
    lefts, rights, results = rest[-3:]
    count = live[0]
    row = pairs[0, 0, 0] // 8
    col = pairs[0, 0, 1] % 8
    z, x, y, c = row // 4, row % 4, col // 2, col % 2

    def row_shift(target):
        dz, dx = (target // 4 - z) & 3, (target % 4 - x) & 3
        return jnp.where(c == 0, dx, dz), jnp.where(c == 0, dz, dx)

    for out in outs:
        out[...] = jnp.zeros_like(out)
    if with_gram:
        gram = merge(g0[0, :, 1024:1152])
        for array in gathered[1:]:
            gram = gram + merge(array[0, :, 1024:1152])
        rest[6][...] = gram
        outs[5][0, :, 1024:1152] = split(gram)

    def advance(slot, carry):
        first, second = pairs[0, slot, 0], pairs[0, slot, 1]
        outer, inner = row_shift(second // 8)
        dy = (first % 8 // 2) ^ y
        dy = dy ^ (dy >> 1)
        dc = (first % 8 % 2) ^ c
        for t in range(4):
            @pl.when((-outer & 3) == t)
            def _():
                lefts[...] = gathered[t][-inner & 3, :, 0:1024]
        for t in range(2):
            @pl.when(dc == t)
            def _():
                rights[...] = pair_gathered[t][dy]
        matrix = blocks[slot]
        direct = lax.dot_general(
            lefts[...], matrix, (((1,), (1,)), ((), ())), preferred_element_type=jnp.float32
        )
        mirror = lax.dot_general(
            rights[...], matrix, (((1,), (0,)), ((), ())), preferred_element_type=jnp.float32
        )
        results[slot, 0] = direct
        results[slot, 1] = jnp.where(first != second, mirror, 0.0)

        def earlier(before, carry):
            @pl.when(pairs[0, before, 0] == first)
            def _():
                lefts_sum = results[3, 0] + results[before, 0]
                results[3, 0] = lefts_sum

            @pl.when(pairs[0, before, 1] == second)
            def _():
                results[3, 1] = results[3, 1] + results[before, 1]

            return carry

        results[3] = results[slot]
        lax.fori_loop(0, slot, earlier, 0)
        for t in range(4):
            @pl.when(outer == t)
            def _():
                outs[t][inner] = results[3, 1].astype(outs[t].dtype)
        for t in range(2):
            @pl.when(dc == t)
            def _():
                outs[4 + t][dy, :, 0:1024] = results[3, 0].astype(outs[4 + t].dtype)
        return carry

    lax.fori_loop(0, count, advance, 0)


def product(pairs, live, blocks, gathered, pair_gathered, sent, with_gram):
    shape = (4, 32, 1024)
    f32 = jnp.float32
    outs = [struct(shape, f32)] + [struct(shape, sent)] * 3 + [struct(shape, f32)]
    outs += [struct((4, 32, 1152) if with_gram else shape, sent)]
    outs += [struct((8, 128), f32)] * with_gram
    return pl.pallas_call(
        functools.partial(product_kernel, with_gram),
        out_shape=outs,
        in_specs=[SMEM, SMEM] + [VMEM] * 7,
        out_specs=[VMEM] * len(outs),
        scratch_shapes=[
            pltpu.VMEM((32, 1024), jnp.bfloat16),
            pltpu.VMEM((32, 1024), jnp.bfloat16),
            pltpu.VMEM((4, 2, 32, 1024), f32),
        ],
        compiler_params=PARAMS,
        cost_estimate=pl.CostEstimate(flops=800_000_000, bytes_accessed=10_000_000, transcendentals=0),
        name="product",
    )(pairs, live, blocks, *gathered, *pair_gathered)


def join_kernel(with_gram, *refs):
    parts, pair, joined, joined_pair = refs[:4], refs[4:6], refs[6], refs[7]
    for k, part in enumerate(parts):
        joined[k] = part[...]
    if with_gram:
        gram = merge(parts[0][:, 1024:1152])
        for part in parts[1:]:
            gram = gram + merge(part[:, 1024:1152])
        joined[0, :, 1024:1152] = split(gram)
    for k, part in enumerate(pair):
        joined_pair[k] = part[...]


def join(parts, pair, with_gram):
    shapes = [(4,) + parts[0].shape, (2,) + pair[0].shape]
    return pl.pallas_call(
        functools.partial(join_kernel, with_gram),
        out_shape=[struct(shape, jnp.bfloat16) for shape in shapes],
        in_specs=[VMEM] * 6,
        out_specs=[VMEM] * 2,
        compiler_params=PARAMS,
        name="join",
    )(*parts, *pair)


def halve_kernel(with_gram, own, received, *rest):
    outs = rest[with_gram:]
    keep, send = outs[:2]
    half = keep.shape[0]
    for k in range(2 * half):
        value = own[k] + received[k, :, 0:1024].astype(jnp.float32)
        if k < half:
            keep[k] = value
        else:
            send[k - half, :, 0:1024] = value.astype(send.dtype)
    if with_gram:
        gram = rest[0][...] + merge(received[0, :, 1024:1152])
        outs[2][...] = gram
        for k in range(half):
            send[k, :, 1024:1152] = split(gram)


def halve(own, received, gram):
    f32 = jnp.float32
    half = own.shape[0] // 2
    outs = [struct((half, 32, 1024), f32), struct((half,) + received.shape[1:], received.dtype)]
    outs += [struct((8, 128), f32)] * len(gram)
    return pl.pallas_call(
        functools.partial(halve_kernel, len(gram)),
        out_shape=outs,
        in_specs=[VMEM] * (2 + len(gram)),
        out_specs=[VMEM] * len(outs),
        compiler_params=PARAMS,
        name="halve",
    )(own, received, *gram)


def row_kernel(own, *refs):
    received, outs = refs[:3], refs[3:]
    for k in range(4):
        value = own[k]
        for array in received:
            value = value + array[k].astype(jnp.float32)
        outs[k][...] = value.astype(outs[k].dtype)


def add_outer(own, received, sent):
    return pl.pallas_call(
        row_kernel,
        out_shape=[struct((32, 1024), jnp.float32)] + [struct((32, 1024), sent)] * 3,
        in_specs=[VMEM] * 4,
        out_specs=[VMEM] * 4,
        compiler_params=PARAMS,
        name="add_outer",
    )(own, *received)


def add_parts(parts):
    value = parts[0][...] + parts[1][0]
    for part in parts[2:5]:
        value = value + part[...].astype(jnp.float32)
    return value + parts[5][0, :, 0:1024].astype(jnp.float32)


def first_kernel(*refs):
    parts, (first, panel, own) = refs[:6], refs[6:]
    value = add_parts(parts)
    first[...] = value
    rounded = value.astype(jnp.bfloat16)
    panel[:, 0:1024] = rounded
    own[...] = rounded
    panel[:, 1024:1152] = split(
        fold(
            lax.dot_general(
                rounded, rounded, (((1,), (1,)), ((), ())), preferred_element_type=jnp.float32
            )
        )
    )


def finish_first(parts):
    return pl.pallas_call(
        first_kernel,
        out_shape=[
            struct((32, 1024), jnp.float32),
            struct((32, 1152), jnp.bfloat16),
            struct((32, 1024), jnp.bfloat16),
        ],
        in_specs=[VMEM] * 6,
        out_specs=[VMEM] * 3,
        compiler_params=PARAMS,
        name="finish_first",
    )(*parts)


def second_kernel(*refs):
    parts, inverse, (scaled, gram) = refs[:6], refs[6], refs[7:]
    value = add_parts(parts)
    value = jnp.dot(inverse[...], value, precision=HIGHEST, preferred_element_type=jnp.float32)
    scaled[...] = value
    tile = fold(
        lax.dot_general(
            value, value, (((1,), (1,)), ((), ())), precision=HIGHEST, preferred_element_type=jnp.float32
        )
    )
    for k in range(8):
        gram[k] = tile


def finish_second(parts, inverse):
    return pl.pallas_call(
        second_kernel,
        out_shape=[struct((32, 1024), jnp.float32), struct((8, 8, 128), jnp.float32)],
        in_specs=[VMEM] * 7,
        out_specs=[VMEM] * 2,
        compiler_params=PARAMS,
        name="finish_second",
    )(*parts, inverse)


def total_kernel(tiles, out):
    total = tiles[0]
    for k in range(1, 8):
        total = total + tiles[k]
    for k in range(16):
        out[k] = total


def total_gram(tiles):
    tiles = lax.all_to_all(tiles, "col", 0, 0, tiled=True)
    tiles = pl.pallas_call(
        total_kernel,
        out_shape=struct((16, 8, 128), jnp.float32),
        in_specs=[VMEM],
        out_specs=VMEM,
        compiler_params=PARAMS,
        name="total_gram",
    )(tiles)
    return lax.all_to_all(tiles, "row", 0, 0, tiled=True)


def lower_inverse(gram):
    rows = lax.broadcasted_iota(jnp.int32, (32, 128), 0)
    lanes = lax.broadcasted_iota(jnp.int32, (32, 128), 1)
    wide = jnp.concatenate([gram, jnp.zeros((32, 96), jnp.float32)], axis=1)
    wide = jnp.where(lanes == rows + 32, 1.0, wide)
    for k in range(31):
        pivot = wide[k : k + 1, k : k + 1]
        factor = jnp.where(rows > k, wide[:, k : k + 1], 0.0)
        wide = wide - factor * (wide[k : k + 1, :] / pivot)
    diagonal = jnp.sum(jnp.where(lanes == rows, wide, 0.0), axis=1, keepdims=True)
    wide = wide / jnp.sqrt(diagonal)
    return wide[:, 32:64]


def factor_kernel(root, gram, panel, *outs):
    tile = gram[0]
    for k in range(1, 16):
        tile = tile + gram[k]
    inverse = lower_inverse(unfold(tile))
    outs[0][...] = (
        jnp.dot(inverse, panel[...], precision=HIGHEST, preferred_element_type=jnp.float32) * root
    )


def factor_first_kernel(root, gram, received, panel, basis, inverse):
    inverse[...] = lower_inverse(unfold(gram[...] + merge(received[0, :, 1024:1152])))
    basis[...] = (
        jnp.dot(inverse[...], panel[...], precision=HIGHEST, preferred_element_type=jnp.float32) * root
    )


def factor_first(gram, received, first, root):
    return pl.pallas_call(
        functools.partial(factor_first_kernel, root),
        out_shape=[struct((32, 1024), jnp.float32), struct((32, 32), jnp.float32)],
        in_specs=[VMEM] * 3,
        out_specs=[VMEM] * 2,
        compiler_params=PARAMS,
        cost_estimate=pl.CostEstimate(flops=1_000_000, bytes_accessed=10_000_000, transcendentals=0),
        name="factor_first",
    )(gram, received, first)


def factor_second(gram, scaled, root):
    return pl.pallas_call(
        functools.partial(factor_kernel, root),
        out_shape=struct((32, 1024), jnp.float32),
        in_specs=[VMEM] * 2,
        out_specs=VMEM,
        compiler_params=PARAMS,
        name="factor_second",
    )(gram, scaled)


SHIFTS = (1, 3, 2)


def spread(send, value):
    got = {s: send(value, s) for s in SHIFTS}
    return [value] + [got[s] for s in (1, 2, 3)]


def gather(panel, own, with_gram):
    inner, pair = join(spread(send_inner, panel), [own, send_y(own, 1)], with_gram)
    outer = spread(send_outer, inner)
    along_y = jnp.concatenate([pair, send_y(pair, 3)])
    return outer, [along_y, send_core(along_y)]


def scatter(parts, sent):
    got = [send_outer(parts[s], s) for s in SHIFTS]
    column, send, *gram = halve(parts[4], send_core(parts[5]), parts[6:])
    column, send, *gram = halve(column, send_y(send, 3), gram)
    along_y = send_y(send, 1)
    row = add_outer(parts[0], got, sent)
    return [row[0], column] + [send_inner(row[s], s) for s in SHIFTS] + [along_y], gram


def hold_kernel(source, target, sem):
    copy = pltpu.make_async_copy(source, target, sem)
    copy.start()
    copy.wait()


def hold(blocks):
    return pl.pallas_call(
        hold_kernel,
        out_shape=struct(blocks.shape, blocks.dtype),
        in_specs=[pl.BlockSpec(memory_space=pl.ANY)],
        out_specs=VMEM,
        scratch_shapes=[pltpu.SemaphoreType.DMA(())],
        compiler_params=PARAMS,
        cost_estimate=pl.CostEstimate(flops=0, bytes_accessed=6_000_000, transcendentals=0),
        name="hold",
    )(blocks)


def on_device(block_pairs, live_counts, pair_blocks, start_basis):
    users = 128 * start_basis.shape[2]
    root = float(users) ** 0.5
    pair_blocks = hold(pair_blocks)
    gathered, pair_gathered = gather(start_basis[0], start_basis[0], False)
    parts = product(block_pairs, live_counts, pair_blocks, gathered, pair_gathered, jnp.float32, False)
    first, panel, own = finish_first(scatter(parts, jnp.float32)[0])
    gathered, pair_gathered = gather(panel, own, True)
    parts = product(block_pairs, live_counts, pair_blocks, gathered, pair_gathered, jnp.bfloat16, True)
    parts, (gram,) = scatter(parts, jnp.bfloat16)
    first_basis, inverse = factor_first(gram, parts[5], first, root)
    scaled, tiles = finish_second(parts, inverse)
    embedding = factor_second(total_gram(tiles), scaled, root)
    return (first_basis[None], embedding[None])


def solution(mesh):
    spec = P(BOTH, None, None)
    return jax.shard_map(
        on_device, mesh=mesh, in_specs=(spec, P(BOTH), spec, spec), out_specs=(spec, spec), check_vma=False
    )
```

```python
import functools

import jax
import jax.numpy as jnp
from jax import lax
from jax.experimental import pallas as pl
from jax.experimental.pallas import tpu as pltpu
from jax.sharding import Mesh
from jax.sharding import PartitionSpec as P

AXES = ("z", "x", "y", "core")
HIGHEST = lax.Precision.HIGHEST
VMEM = pl.BlockSpec(memory_space=pltpu.VMEM)
SMEM = pl.BlockSpec(memory_space=pltpu.SMEM)
PARAMS = pltpu.CompilerParams(vmem_limit_bytes=24 * 1024 * 1024)


def permute(value, target):
    pairs = []
    for device in range(128):
        z, x, y, c = device // 32, device // 8 % 4, device // 2 % 4, device % 2
        tz, tx, ty, tc = target(z, x, y, c)
        pairs.append((device, ((tz % 4) * 4 + tx % 4) * 8 + (ty % 4) * 2 + tc % 2))
    return lax.ppermute(value, AXES, pairs)


def send_inner(value, s):
    return permute(value, lambda z, x, y, c: (z + s, x, y, c) if c == 0 else (z, x + s, y, c))


def send_outer(value, s):
    return permute(value, lambda z, x, y, c: (z, x + s, y, c) if c == 0 else (z + s, x, y, c))


def send_y(value, s):
    return permute(value, lambda z, x, y, c: (z, x, y ^ s, c))


def send_core(value):
    return permute(value, lambda z, x, y, c: (z, x, y, c + 1))


def struct(shape, dtype):
    return jax.ShapeDtypeStruct(shape, dtype)


def fold(gram):
    return jnp.concatenate([gram[8 * k : 8 * k + 8] for k in range(4)], axis=1)


def unfold(tile):
    return jnp.concatenate([tile[:, 32 * k : 32 * k + 32] for k in range(4)], axis=0)


def split(tile):
    terms = []
    for _ in range(3):
        term = tile.astype(jnp.bfloat16).astype(jnp.float32)
        terms.append(term)
        tile = tile - term
    return jnp.concatenate(terms + [jnp.zeros_like(tile)], axis=0).astype(jnp.bfloat16)


def encode(value):
    top = jnp.max(jnp.abs(value), axis=1, keepdims=True)
    power = jnp.floor(jnp.log2(jnp.maximum(top, 1e-30))) - 13.0
    return jnp.concatenate([value * jnp.exp2(-power), jnp.broadcast_to(power, (32, 128))], axis=1)


def decode(value):
    if value.dtype == jnp.bfloat16:
        return value[:, 0:1024].astype(jnp.float32)
    return value[:, 0:1024] * jnp.exp2(value[:, 1024:1025])


def carry(send, value, *args):
    if value.dtype == jnp.bfloat16:
        return send(value, *args)
    return send(value.astype(jnp.float16), *args).astype(jnp.float32)


def merge(terms):
    terms = terms.astype(jnp.float32)
    return terms[0:8] + terms[8:16] + terms[16:24]


def product_kernel(with_gram, pairs, live, blocks, g0, g1, g2, g3, h0, h1, *rest):
    gathered, pair_gathered = (g0, g1, g2, g3), (h0, h1)
    outs = rest[:6]
    lefts, rights, results = rest[-3:]
    count = live[0]
    row = pairs[0, 0, 0] // 8
    col = pairs[0, 0, 1] % 8
    z, x, y, c = row // 4, row % 4, col // 2, col % 2

    def row_shift(target):
        dz, dx = (target // 4 - z) & 3, (target % 4 - x) & 3
        return jnp.where(c == 0, dx, dz), jnp.where(c == 0, dz, dx)

    for out in outs:
        out[...] = jnp.zeros_like(out)
    if with_gram:
        gram = merge(g0[0, :, 1024:1152])
        for array in gathered[1:]:
            gram = gram + merge(array[0, :, 1024:1152])
        rest[6][...] = gram
        outs[5][0, :, 1024:1152] = split(gram)

    def advance(slot, carry):
        first, second = pairs[0, slot, 0], pairs[0, slot, 1]
        outer, inner = row_shift(second // 8)
        dy = (first % 8 // 2) ^ y
        dy = dy ^ (dy >> 1)
        dc = (first % 8 % 2) ^ c
        for t in range(4):
            @pl.when((-outer & 3) == t)
            def _():
                lefts[...] = gathered[t][-inner & 3, :, 0:1024]
        for t in range(2):
            @pl.when(dc == t)
            def _():
                rights[...] = pair_gathered[t][dy]
        matrix = blocks[slot]
        direct = lax.dot_general(
            lefts[...], matrix, (((1,), (1,)), ((), ())), preferred_element_type=jnp.float32
        )
        mirror = lax.dot_general(
            rights[...], matrix, (((1,), (0,)), ((), ())), preferred_element_type=jnp.float32
        )
        results[slot, 0] = direct
        results[slot, 1] = jnp.where(first != second, mirror, 0.0)

        def earlier(before, carry):
            @pl.when(pairs[0, before, 0] == first)
            def _():
                lefts_sum = results[3, 0] + results[before, 0]
                results[3, 0] = lefts_sum

            @pl.when(pairs[0, before, 1] == second)
            def _():
                results[3, 1] = results[3, 1] + results[before, 1]

            return carry

        results[3] = results[slot]
        lax.fori_loop(0, slot, earlier, 0)
        for t in range(4):
            @pl.when(outer == t)
            def _():
                if t and not with_gram:
                    outs[t][inner] = encode(results[3, 1])
                else:
                    outs[t][inner] = results[3, 1].astype(outs[t].dtype)
        for t in range(2):
            @pl.when(dc == t)
            def _():
                if t and not with_gram:
                    outs[5][dy] = encode(results[3, 0])
                else:
                    outs[4 + t][dy, :, 0:1024] = results[3, 0].astype(outs[4 + t].dtype)
        return carry

    lax.fori_loop(0, count, advance, 0)


def product(pairs, live, blocks, gathered, pair_gathered, with_gram):
    shape = (4, 32, 1024)
    f32 = jnp.float32
    sent = jnp.bfloat16 if with_gram else f32
    outs = [struct(shape, f32)] + [struct(shape if with_gram else (4, 32, 1152), sent)] * 3
    outs += [struct(shape, f32), struct((4, 32, 1152), sent)]
    outs += [struct((8, 128), f32)] * with_gram
    return pl.pallas_call(
        functools.partial(product_kernel, with_gram),
        out_shape=outs,
        in_specs=[SMEM, SMEM] + [VMEM] * 7,
        out_specs=[VMEM] * len(outs),
        scratch_shapes=[
            pltpu.VMEM((32, 1024), jnp.bfloat16),
            pltpu.VMEM((32, 1024), jnp.bfloat16),
            pltpu.VMEM((4, 2, 32, 1024), f32),
        ],
        compiler_params=PARAMS,
        cost_estimate=pl.CostEstimate(flops=800_000_000, bytes_accessed=10_000_000, transcendentals=0),
        name="product",
    )(pairs, live, blocks, *gathered, *pair_gathered)


def join_kernel(with_gram, *refs):
    parts, pair, joined, joined_pair = refs[:4], refs[4:6], refs[6], refs[7]
    for k, part in enumerate(parts):
        joined[k] = part[...]
    if with_gram:
        gram = merge(parts[0][:, 1024:1152])
        for part in parts[1:]:
            gram = gram + merge(part[:, 1024:1152])
        joined[0, :, 1024:1152] = split(gram)
    for k, part in enumerate(pair):
        joined_pair[k] = part[...]


def join(parts, pair, with_gram):
    shapes = [(4,) + parts[0].shape, (2,) + pair[0].shape]
    return pl.pallas_call(
        functools.partial(join_kernel, with_gram),
        out_shape=[struct(shape, jnp.bfloat16) for shape in shapes],
        in_specs=[VMEM] * 6,
        out_specs=[VMEM] * 2,
        compiler_params=PARAMS,
        name="join",
    )(*parts, *pair)


def halve_kernel(with_gram, own, received, *rest):
    outs = rest[with_gram:]
    keep, send = outs[:2]
    half = keep.shape[0]
    for k in range(2 * half):
        value = own[k] + decode(received[k])
        if k < half:
            keep[k] = value
        elif not with_gram:
            send[k - half] = encode(value)
        else:
            send[k - half, :, 0:1024] = value.astype(send.dtype)
    if with_gram:
        gram = rest[0][...] + merge(received[0, :, 1024:1152])
        outs[2][...] = gram
        for k in range(half):
            send[k, :, 1024:1152] = split(gram)


def halve(own, received, gram):
    f32 = jnp.float32
    half = own.shape[0] // 2
    outs = [struct((half, 32, 1024), f32), struct((half,) + received.shape[1:], received.dtype)]
    outs += [struct((8, 128), f32)] * len(gram)
    return pl.pallas_call(
        functools.partial(halve_kernel, len(gram)),
        out_shape=outs,
        in_specs=[VMEM] * (2 + len(gram)),
        out_specs=[VMEM] * len(outs),
        compiler_params=PARAMS,
        name="halve",
    )(own, received, *gram)


def row_kernel(own, *refs):
    received, outs = refs[:3], refs[3:]
    for k in range(4):
        value = own[k]
        for array in received:
            value = value + decode(array[k])
        if outs[k].shape[1] > 1024:
            value = encode(value)
        outs[k][...] = value.astype(outs[k].dtype)


def add_outer(own, received):
    sent = struct(received[0].shape[1:], received[0].dtype)
    return pl.pallas_call(
        row_kernel,
        out_shape=[struct((32, 1024), jnp.float32)] + [sent] * 3,
        in_specs=[VMEM] * 4,
        out_specs=[VMEM] * 4,
        compiler_params=PARAMS,
        name="add_outer",
    )(own, *received)


def add_parts(parts):
    value = parts[0][...] + parts[1][0]
    for part in parts[2:5]:
        value = value + decode(part[...])
    return value + decode(parts[5][0])


def first_kernel(*refs):
    parts, (first, panel, own) = refs[:6], refs[6:]
    value = add_parts(parts)
    first[...] = value
    rounded = value.astype(jnp.bfloat16)
    panel[:, 0:1024] = rounded
    own[...] = rounded
    panel[:, 1024:1152] = split(
        fold(
            lax.dot_general(
                rounded, rounded, (((1,), (1,)), ((), ())), preferred_element_type=jnp.float32
            )
        )
    )


def finish_first(parts):
    return pl.pallas_call(
        first_kernel,
        out_shape=[
            struct((32, 1024), jnp.float32),
            struct((32, 1152), jnp.bfloat16),
            struct((32, 1024), jnp.bfloat16),
        ],
        in_specs=[VMEM] * 6,
        out_specs=[VMEM] * 3,
        compiler_params=PARAMS,
        name="finish_first",
    )(*parts)


def second_kernel(*refs):
    parts, inverse, (scaled, gram) = refs[:6], refs[6], refs[7:]
    value = add_parts(parts)
    value = jnp.dot(inverse[...], value, precision=HIGHEST, preferred_element_type=jnp.float32)
    scaled[...] = value
    tile = fold(
        lax.dot_general(
            value, value, (((1,), (1,)), ((), ())), precision=HIGHEST, preferred_element_type=jnp.float32
        )
    )
    gram[...] = tile


def finish_second(parts, inverse):
    return pl.pallas_call(
        second_kernel,
        out_shape=[struct((32, 1024), jnp.float32), struct((8, 128), jnp.float32)],
        in_specs=[VMEM] * 7,
        out_specs=[VMEM] * 2,
        compiler_params=PARAMS,
        name="finish_second",
    )(*parts, inverse)


def total_kernel(own, other, out):
    total = own[...] + other[...]
    for k in range(64):
        out[k] = total


def total_gram(tile):
    tiles = pl.pallas_call(
        total_kernel,
        out_shape=struct((64, 8, 128), jnp.float32),
        in_specs=[VMEM] * 2,
        out_specs=VMEM,
        compiler_params=PARAMS,
        name="total_gram",
    )(tile, send_core(tile))
    return lax.all_to_all(tiles, ("z", "x", "y"), 0, 0, tiled=True)


def lower_inverse(gram):
    rows = lax.broadcasted_iota(jnp.int32, (32, 128), 0)
    lanes = lax.broadcasted_iota(jnp.int32, (32, 128), 1)
    wide = jnp.concatenate([gram, jnp.zeros((32, 96), jnp.float32)], axis=1)
    wide = jnp.where(lanes == rows + 32, 1.0, wide)
    parts = [wide[8 * k : 8 * k + 8] for k in range(4)]
    inside = rows[0:8]
    for step in range(4):
        columns = [
            [jnp.broadcast_to(part[:, k : k + 1], (8, 128)) for k in range(8 * step, 8 * step + 8)]
            for part in parts
        ]
        pivot = parts[step]
        schur = {(i, j): columns[step][j][i : i + 1] for i in range(8) for j in range(i + 1)}
        lines = [pivot[i : i + 1] for i in range(8)]
        factors, inverses = {}, []
        for j in range(8):
            inverses.append(1.0 / schur[j, j])
            for i in range(j + 1, 8):
                factors[i, j] = schur[i, j] * inverses[j]
            for i in range(j + 1, 8):
                for t in range(j + 1, i + 1):
                    schur[i, t] = schur[i, t] - factors[i, j] * schur[t, j]
                lines[i] = lines[i] - factors[i, j] * lines[j]
        for i in range(1, 8):
            pivot = jnp.where(inside == i, lines[i], pivot)
        parts[step] = pivot
        solved = [None] * 8
        for j in reversed(range(8)):
            value = lines[j] * inverses[j]
            for i in range(j + 1, 8):
                value = value - factors[i, j] * solved[i]
            solved[j] = value
        for later in range(step + 1, 4):
            for j in range(8):
                parts[later] = parts[later] - columns[later][j] * solved[j]
    wide = jnp.concatenate(parts, axis=0)
    diagonal = jnp.sum(jnp.where(lanes == rows, wide, 0.0), axis=1, keepdims=True)
    wide = wide / jnp.sqrt(diagonal)
    return wide[:, 32:64]


def factor_kernel(root, gram, panel, *outs):
    tile = gram[0]
    for k in range(1, 64):
        tile = tile + gram[k]
    inverse = lower_inverse(unfold(tile))
    outs[0][...] = (
        jnp.dot(inverse, panel[...], precision=HIGHEST, preferred_element_type=jnp.float32) * root
    )


def factor_first_kernel(root, gram, received, panel, basis, inverse):
    inverse[...] = lower_inverse(unfold(gram[...] + merge(received[0, :, 1024:1152])))
    basis[...] = (
        jnp.dot(inverse[...], panel[...], precision=HIGHEST, preferred_element_type=jnp.float32) * root
    )


def factor_first(gram, received, first, root):
    return pl.pallas_call(
        functools.partial(factor_first_kernel, root),
        out_shape=[struct((32, 1024), jnp.float32), struct((32, 32), jnp.float32)],
        in_specs=[VMEM] * 3,
        out_specs=[VMEM] * 2,
        compiler_params=PARAMS,
        cost_estimate=pl.CostEstimate(flops=1_000_000, bytes_accessed=10_000_000, transcendentals=0),
        name="factor_first",
    )(gram, received, first)


def factor_second(gram, scaled, root):
    return pl.pallas_call(
        functools.partial(factor_kernel, root),
        out_shape=struct((32, 1024), jnp.float32),
        in_specs=[VMEM] * 2,
        out_specs=VMEM,
        compiler_params=PARAMS,
        name="factor_second",
    )(gram, scaled)


SHIFTS = (1, 3, 2)


def spread(send, value):
    got = {s: send(value, s) for s in SHIFTS}
    return [value] + [got[s] for s in (1, 2, 3)]


def gather(panel, own, with_gram):
    inner, pair = join(spread(send_inner, panel), [own, send_y(own, 1)], with_gram)
    outer = spread(send_outer, inner)
    along_y = jnp.concatenate([pair, send_y(pair, 3)])
    return outer, [along_y, send_core(along_y)]


def scatter(parts):
    got = [carry(send_outer, parts[s], s) for s in SHIFTS]
    column, send, *gram = halve(parts[4], carry(send_core, parts[5]), parts[6:])
    column, send, *gram = halve(column, carry(send_y, send, 3), gram)
    along_y = carry(send_y, send, 1)
    row = add_outer(parts[0], got)
    return [row[0], column] + [carry(send_inner, row[s], s) for s in SHIFTS] + [along_y], gram


def hold_kernel(source, target, sem):
    copy = pltpu.make_async_copy(source, target, sem)
    copy.start()
    copy.wait()


def hold(blocks):
    return pl.pallas_call(
        hold_kernel,
        out_shape=struct(blocks.shape, blocks.dtype),
        in_specs=[pl.BlockSpec(memory_space=pl.ANY)],
        out_specs=VMEM,
        scratch_shapes=[pltpu.SemaphoreType.DMA(())],
        compiler_params=PARAMS,
        cost_estimate=pl.CostEstimate(flops=0, bytes_accessed=6_000_000, transcendentals=0),
        name="hold",
    )(blocks)


def on_device(block_pairs, live_counts, pair_blocks, start_basis):
    users = 128 * start_basis.shape[2]
    root = float(users) ** 0.5
    pair_blocks = hold(pair_blocks)
    gathered, pair_gathered = gather(start_basis[0], start_basis[0], False)
    parts = product(block_pairs, live_counts, pair_blocks, gathered, pair_gathered, False)
    first, panel, own = finish_first(scatter(parts)[0])
    gathered, pair_gathered = gather(panel, own, True)
    parts = product(block_pairs, live_counts, pair_blocks, gathered, pair_gathered, True)
    parts, (gram,) = scatter(parts)
    first_basis, inverse = factor_first(gram, parts[5], first, root)
    scaled, tiles = finish_second(parts, inverse)
    embedding = factor_second(total_gram(tiles), scaled, root)
    return (first_basis[None], embedding[None])


def solution(mesh):
    mesh = Mesh(mesh.devices.reshape(4, 4, 4, 2), AXES)
    spec = P(AXES, None, None)
    return jax.shard_map(
        on_device, mesh=mesh, in_specs=(spec, P(AXES), spec, spec), out_specs=(spec, spec), check_vma=False
    )
```

```python
import functools

import jax
import jax.numpy as jnp
from jax import lax
from jax.experimental import pallas as pl
from jax.experimental.pallas import tpu as pltpu
from jax.sharding import Mesh
from jax.sharding import PartitionSpec as P

AXES = ("z", "x", "y", "core")
HIGHEST = lax.Precision.HIGHEST
VMEM = pl.BlockSpec(memory_space=pltpu.VMEM)
SMEM = pl.BlockSpec(memory_space=pltpu.SMEM)
PARAMS = pltpu.CompilerParams(vmem_limit_bytes=24 * 1024 * 1024)


def permute(value, target):
    pairs = []
    for device in range(128):
        z, x, y, c = device // 32, device // 8 % 4, device // 2 % 4, device % 2
        tz, tx, ty, tc = target(z, x, y, c)
        pairs.append((device, ((tz % 4) * 4 + tx % 4) * 8 + (ty % 4) * 2 + tc % 2))
    return lax.ppermute(value, AXES, pairs)


def send_inner(value, s):
    return permute(value, lambda z, x, y, c: (z + s, x, y, c) if c == 0 else (z, x + s, y, c))


def send_outer(value, s):
    return permute(value, lambda z, x, y, c: (z, x + s, y, c) if c == 0 else (z + s, x, y, c))


def send_y(value, s):
    return permute(value, lambda z, x, y, c: (z, x, y ^ s if c == 0 else y ^ (4 - s), c))


def send_core(value):
    return permute(value, lambda z, x, y, c: (z, x, y, c + 1))


def struct(shape, dtype):
    return jax.ShapeDtypeStruct(shape, dtype)


def fold(gram):
    return jnp.concatenate([gram[8 * k : 8 * k + 8] for k in range(4)], axis=1)


def unfold(tile):
    return jnp.concatenate([tile[:, 32 * k : 32 * k + 32] for k in range(4)], axis=0)


def split(tile):
    terms = []
    for _ in range(3):
        term = tile.astype(jnp.bfloat16).astype(jnp.float32)
        terms.append(term)
        tile = tile - term
    return jnp.concatenate(terms + [jnp.zeros_like(tile)], axis=0).astype(jnp.bfloat16)


def encode(value):
    top = jnp.max(jnp.abs(value), axis=1, keepdims=True)
    power = jnp.floor(jnp.log2(jnp.maximum(top, 1e-30))) - 13.0
    return jnp.concatenate([value * jnp.exp2(-power), jnp.broadcast_to(power, (32, 128))], axis=1)


def decode(value):
    if value.dtype == jnp.bfloat16:
        return value[:, 0:1024].astype(jnp.float32)
    return value[:, 0:1024] * jnp.exp2(value[:, 1024:1025])


def put(ref, k, value):
    for i in range(2):
        for j in range(8):
            ref[16 * k + 8 * i + j] = value[16 * i : 16 * i + 16, 128 * j : 128 * j + 128]


def take(ref, k):
    rows = [jnp.concatenate([ref[16 * k + 8 * i + j] for j in range(8)], axis=1) for i in range(2)]
    return jnp.concatenate(rows, axis=0)


def take_extra(ref, k):
    return jnp.concatenate([ref[16 * k], ref[16 * k + 1]], axis=0)


def put_extra(ref, k, value):
    ref[16 * k] = value[0:16]
    ref[16 * k + 1] = value[16:32]


def carry(send, value, *args):
    if value.dtype == jnp.bfloat16:
        return send(value, *args)
    return send(value.astype(jnp.float16), *args).astype(jnp.float32)


def merge(terms):
    terms = terms.astype(jnp.float32)
    return terms[0:8] + terms[8:16] + terms[16:24]


def places(pairs, slot):
    first, second = pairs[0, slot, 0], pairs[0, slot, 1]
    row, col = first // 8, second % 8
    dz, dx = (second // 8 // 4 - row // 4) & 3, (second // 8 % 4 - row % 4) & 3
    c = col % 2
    outer, inner = jnp.where(c == 0, dx, dz), jnp.where(c == 0, dz, dx)
    dy = (first % 8 // 2) ^ (col // 2)
    dy = dy ^ (dy >> 1)
    dy = jnp.where(first % 2 == 0, dy, (dy & 1) * 2 + (dy >> 1))
    return outer, inner, (first % 2) ^ c, dy


def load_right(pairs, slot, pair_gathered, rights):
    outer, inner, dc, dy = places(pairs, slot)
    for t in range(2):
        @pl.when(dc == t)
        def _():
            rights[...] = pair_gathered[t][dy]


def load_left(pairs, slot, gathered, lefts):
    outer, inner, dc, dy = places(pairs, slot)
    for t in range(4):
        @pl.when((-outer & 3) == t)
        def _():
            lefts[...] = take(gathered[t], -inner & 3)


def multiply(panel, matrix):
    return jnp.dot(panel[...], matrix, preferred_element_type=jnp.float32)


def store_mirror(pairs, slot, value, outs, half):
    outer, inner, dc, dy = places(pairs, slot)
    value = jnp.where(pairs[0, slot, 0] != pairs[0, slot, 1], value, 0.0)
    lanes = lax.broadcasted_iota(jnp.int32, (32, 128), 1)

    @pl.when(outer == 0)
    def _():
        outs[0][inner] = outs[0][inner] + value

    for t in range(1, 4):
        @pl.when(outer == t)
        def _():
            place = jnp.where(lanes == 8 * slot + inner, 1.0, 0.0)
            if half:
                coded = encode(value)
                put(outs[t], slot, coded[:, 0:1024])
                place = place + jnp.where(lanes == 8 * slot + 4, coded[:, 1024:1152], 0.0)
            else:
                put(outs[t], slot, value.astype(jnp.bfloat16))
            extra = take_extra(outs[t], 3).astype(jnp.float32) + place
            put_extra(outs[t], 3, extra.astype(outs[t].dtype))


def store_direct(pairs, slot, value, outs, results, half):
    outer, inner, dc, dy = places(pairs, slot)
    results[slot] = value
    results[3] = value

    def earlier(before, carry):
        @pl.when(pairs[0, before, 0] == pairs[0, slot, 0])
        def _():
            results[3] = results[3] + results[before]

        return carry

    lax.fori_loop(0, slot, earlier, 0)
    for t in range(2):
        @pl.when(dc == t)
        def _():
            if t and half:
                outs[1][dy] = encode(results[3])
            else:
                outs[t][dy, :, 0:1024] = results[3].astype(outs[t].dtype)


def add_gram(gathered, out, sent):
    gram = merge(take_extra(gathered[0], 4))
    for array in gathered[1:]:
        gram = gram + merge(take_extra(array, 4))
    out[...] = gram
    sent[0, :, 1024:1152] = split(gram)


def clear(outs):
    for out in outs:
        out[...] = jnp.zeros_like(out)


def both_kernel(pairs, live, blocks, turned, g0, g1, g2, g3, h0, h1, *rest):
    outs, (lefts, rights, results) = rest[:6], rest[6:]
    clear(outs)

    def advance(slot, carry):
        load_left(pairs, slot, (g0, g1, g2, g3), lefts)
        load_right(pairs, slot, (h0, h1), rights)
        direct = multiply(lefts, turned[slot])
        mirror = multiply(rights, blocks[slot])
        store_direct(pairs, slot, direct, outs[4:], results, True)
        store_mirror(pairs, slot, mirror, outs, True)
        return carry

    lax.fori_loop(0, live[0], advance, 0)


def mirror_kernel(pairs, live, blocks, h0, h1, *rest):
    outs, (rights,) = rest[:4], rest[4:]
    clear(outs)

    def advance(slot, carry):
        load_right(pairs, slot, (h0, h1), rights)
        store_mirror(pairs, slot, multiply(rights, blocks[slot]), outs, False)
        return carry

    lax.fori_loop(0, live[0], advance, 0)


def direct_kernel(pairs, live, turned, g0, g1, g2, g3, after, *rest):
    outs, (lefts, results) = rest[:3], rest[3:]
    clear(outs[:2])
    add_gram((g0, g1, g2, g3), outs[2], outs[1])

    def advance(slot, carry):
        load_left(pairs, slot, (g0, g1, g2, g3), lefts)
        store_direct(pairs, slot, multiply(lefts, turned[slot]), outs, results, False)
        return carry

    lax.fori_loop(0, live[0], advance, 0)


PANEL = pltpu.VMEM((32, 1024), jnp.bfloat16)
RESULTS = pltpu.VMEM((4, 32, 1024), jnp.float32)


def product_call(kernel, outs, scratch, name, pairs, live, *arrays):
    return pl.pallas_call(
        kernel,
        out_shape=outs,
        in_specs=[SMEM, SMEM] + [VMEM] * len(arrays),
        out_specs=[VMEM] * len(outs),
        scratch_shapes=scratch,
        compiler_params=PARAMS,
        name=name,
    )(pairs, live, *arrays)


def first_product(pairs, live, blocks, turned, gathered, pair_gathered):
    f32 = jnp.float32
    outs = [struct((4, 32, 1024), f32)] + [struct((50, 16, 128), f32)] * 3
    outs += [struct((4, 32, 1024), f32), struct((4, 32, 1152), f32)]
    arrays = (blocks, turned, *gathered, *pair_gathered)
    return product_call(both_kernel, outs, [PANEL, PANEL, RESULTS], "product", pairs, live, *arrays)


def second_product(pairs, live, blocks, turned, gathered, pair_gathered):
    f32, bf16 = jnp.float32, jnp.bfloat16
    outs = [struct((4, 32, 1024), f32)] + [struct((50, 16, 128), bf16)] * 3
    rows = product_call(mirror_kernel, outs, [PANEL], "mirror", pairs, live, blocks, *pair_gathered)
    outs = [struct((4, 32, 1024), f32), struct((4, 32, 1152), bf16), struct((8, 128), f32)]
    arrays = (turned, *gathered, rows[0])
    return rows + product_call(direct_kernel, outs, [PANEL, RESULTS], "direct", pairs, live, *arrays)


def join_kernel(with_gram, *refs):
    parts, pair, joined, joined_pair = refs[:4], refs[4:6], refs[6], refs[7]
    for k, part in enumerate(parts):
        put(joined, k, part[:, 0:1024])
    if with_gram:
        gram = merge(parts[0][:, 1024:1152])
        for part in parts[1:]:
            gram = gram + merge(part[:, 1024:1152])
        put_extra(joined, 4, split(gram))
    for k, part in enumerate(pair):
        joined_pair[k] = part[...]


def join(parts, pair, with_gram):
    shapes = [(66 if with_gram else 64, 16, 128), (2,) + pair[0].shape]
    return pl.pallas_call(
        functools.partial(join_kernel, with_gram),
        out_shape=[struct(shape, jnp.bfloat16) for shape in shapes],
        in_specs=[VMEM] * 6,
        out_specs=[VMEM] * 2,
        compiler_params=PARAMS,
        name="join",
    )(*parts, *pair)


def halve_kernel(with_gram, own, received, *rest):
    outs = rest[with_gram:]
    keep, send = outs[:2]
    half = keep.shape[0]
    for k in range(2 * half):
        value = own[k] + decode(received[k])
        if k < half:
            keep[k] = value
        elif not with_gram:
            send[k - half] = encode(value)
        else:
            send[k - half, :, 0:1024] = value.astype(send.dtype)
    if with_gram:
        gram = rest[0][...] + merge(received[0, :, 1024:1152])
        outs[2][...] = gram
        for k in range(half):
            send[k, :, 1024:1152] = split(gram)


def halve(own, received, gram):
    f32 = jnp.float32
    half = own.shape[0] // 2
    outs = [struct((half, 32, 1024), f32), struct((half,) + received.shape[1:], received.dtype)]
    outs += [struct((8, 128), f32)] * len(gram)
    return pl.pallas_call(
        functools.partial(halve_kernel, len(gram)),
        out_shape=outs,
        in_specs=[VMEM] * (2 + len(gram)),
        out_specs=[VMEM] * len(outs),
        compiler_params=PARAMS,
        name="halve",
    )(own, received, *gram)


def row_kernel(half, own, *refs):
    received, outs, (weights, total) = refs[:3], refs[3:7], refs[7:]
    entries = [(array, k) for array in received for k in range(3)]
    extras = [take_extra(array, 3).astype(jnp.float32) for array in received]
    for e, (array, k) in enumerate(entries):
        extra = extras[e // 3]
        scale = jnp.exp2(extra[:, 8 * k + 4 : 8 * k + 5]) if half else 1.0
        for s in range(4):
            weights[4 * e + s] = jnp.broadcast_to(extra[:, 8 * k + s : 8 * k + s + 1] * scale, (32, 128))
    for i in range(2):
        rows = slice(16 * i, 16 * i + 16)
        for j in range(8):
            columns = slice(128 * j, 128 * j + 128)
            sums = [own[s, rows, columns] for s in range(4)]
            for e, (array, k) in enumerate(entries):
                value = array[16 * k + 8 * i + j].astype(jnp.float32)
                for s in range(4):
                    sums[s] = sums[s] + value * weights[4 * e + s, rows]
            for s in range(4):
                total[s, rows, columns] = sums[s]
    outs[0][...] = total[0]
    for s in range(1, 4):
        outs[s][...] = encode(total[s]) if half else total[s].astype(outs[s].dtype)


def add_outer(own, received):
    half = received[0].dtype == jnp.float32
    sent = struct((32, 1152), jnp.float32) if half else struct((32, 1024), jnp.bfloat16)
    return pl.pallas_call(
        functools.partial(row_kernel, half),
        out_shape=[struct((32, 1024), jnp.float32)] + [sent] * 3,
        in_specs=[VMEM] * 4,
        out_specs=[VMEM] * 4,
        scratch_shapes=[pltpu.VMEM((36, 32, 128), jnp.float32), pltpu.VMEM((4, 32, 1024), jnp.float32)],
        compiler_params=PARAMS,
        name="add_outer",
    )(own, *received)


def add_parts(parts):
    value = parts[0][...] + parts[1][0]
    for part in parts[2:5]:
        value = value + decode(part[...])
    return value + decode(parts[5][0])


def first_kernel(*refs):
    parts, (first, panel, own) = refs[:6], refs[6:]
    value = add_parts(parts)
    first[...] = value
    rounded = value.astype(jnp.bfloat16)
    panel[:, 0:1024] = rounded
    own[...] = rounded
    panel[:, 1024:1152] = split(
        fold(
            lax.dot_general(
                rounded, rounded, (((1,), (1,)), ((), ())), preferred_element_type=jnp.float32
            )
        )
    )


def finish_first(parts):
    return pl.pallas_call(
        first_kernel,
        out_shape=[
            struct((32, 1024), jnp.float32),
            struct((32, 1152), jnp.bfloat16),
            struct((32, 1024), jnp.bfloat16),
        ],
        in_specs=[VMEM] * 6,
        out_specs=[VMEM] * 3,
        compiler_params=PARAMS,
        name="finish_first",
    )(*parts)


def second_kernel(*refs):
    parts, inverse, (scaled, gram) = refs[:6], refs[6], refs[7:]
    value = add_parts(parts)
    value = jnp.dot(inverse[...], value, precision=HIGHEST, preferred_element_type=jnp.float32)
    scaled[...] = value
    tile = fold(
        lax.dot_general(
            value, value, (((1,), (1,)), ((), ())), precision=HIGHEST, preferred_element_type=jnp.float32
        )
    )
    gram[...] = tile


def finish_second(parts, inverse):
    return pl.pallas_call(
        second_kernel,
        out_shape=[struct((32, 1024), jnp.float32), struct((8, 128), jnp.float32)],
        in_specs=[VMEM] * 7,
        out_specs=[VMEM] * 2,
        compiler_params=PARAMS,
        name="finish_second",
    )(*parts, inverse)


def total_kernel(own, other, out):
    total = own[...] + other[...]
    for k in range(64):
        out[k] = total


def total_gram(tile):
    tiles = pl.pallas_call(
        total_kernel,
        out_shape=struct((64, 8, 128), jnp.float32),
        in_specs=[VMEM] * 2,
        out_specs=VMEM,
        compiler_params=PARAMS,
        name="total_gram",
    )(tile, send_core(tile))
    return lax.all_to_all(tiles, ("z", "x", "y"), 0, 0, tiled=True)


def lower_inverse(gram):
    rows = lax.broadcasted_iota(jnp.int32, (32, 128), 0)
    lanes = lax.broadcasted_iota(jnp.int32, (32, 128), 1)
    wide = jnp.concatenate([gram, jnp.zeros((32, 96), jnp.float32)], axis=1)
    wide = jnp.where(lanes == rows + 32, 1.0, wide)
    parts = [wide[8 * k : 8 * k + 8] for k in range(4)]
    inside = rows[0:8]
    for step in range(4):
        columns = [
            [jnp.broadcast_to(part[:, k : k + 1], (8, 128)) for k in range(8 * step, 8 * step + 8)]
            for part in parts
        ]
        pivot = parts[step]
        schur = {(i, j): columns[step][j][i : i + 1] for i in range(8) for j in range(i + 1)}
        lines = [pivot[i : i + 1] for i in range(8)]
        factors, inverses = {}, []
        for j in range(8):
            inverses.append(1.0 / schur[j, j])
            for i in range(j + 1, 8):
                factors[i, j] = schur[i, j] * inverses[j]
            for i in range(j + 1, 8):
                for t in range(j + 1, i + 1):
                    schur[i, t] = schur[i, t] - factors[i, j] * schur[t, j]
                lines[i] = lines[i] - factors[i, j] * lines[j]
        for i in range(1, 8):
            pivot = jnp.where(inside == i, lines[i], pivot)
        parts[step] = pivot
        solved = [None] * 8
        for j in reversed(range(8)):
            value = lines[j] * inverses[j]
            for i in range(j + 1, 8):
                value = value - factors[i, j] * solved[i]
            solved[j] = value
        for later in range(step + 1, 4):
            for j in range(8):
                parts[later] = parts[later] - columns[later][j] * solved[j]
    wide = jnp.concatenate(parts, axis=0)
    diagonal = jnp.sum(jnp.where(lanes == rows, wide, 0.0), axis=1, keepdims=True)
    wide = wide / jnp.sqrt(diagonal)
    return wide[:, 32:64]


def factor_kernel(root, gram, panel, *outs):
    tile = gram[0]
    for k in range(1, 64):
        tile = tile + gram[k]
    inverse = lower_inverse(unfold(tile))
    outs[0][...] = (
        jnp.dot(inverse, panel[...], precision=HIGHEST, preferred_element_type=jnp.float32) * root
    )


def factor_first_kernel(root, gram, received, panel, basis, inverse):
    inverse[...] = lower_inverse(unfold(gram[...] + merge(received[0, :, 1024:1152])))
    basis[...] = (
        jnp.dot(inverse[...], panel[...], precision=HIGHEST, preferred_element_type=jnp.float32) * root
    )


def factor_first(gram, received, first, root):
    return pl.pallas_call(
        functools.partial(factor_first_kernel, root),
        out_shape=[struct((32, 1024), jnp.float32), struct((32, 32), jnp.float32)],
        in_specs=[VMEM] * 3,
        out_specs=[VMEM] * 2,
        compiler_params=PARAMS,
        cost_estimate=pl.CostEstimate(flops=1_000_000, bytes_accessed=10_000_000, transcendentals=0),
        name="factor_first",
    )(gram, received, first)


def factor_second(gram, scaled, root):
    return pl.pallas_call(
        functools.partial(factor_kernel, root),
        out_shape=struct((32, 1024), jnp.float32),
        in_specs=[VMEM] * 2,
        out_specs=VMEM,
        compiler_params=PARAMS,
        name="factor_second",
    )(gram, scaled)


SHIFTS = (1, 3, 2)


def spread(send, value):
    got = {s: send(value, s) for s in SHIFTS}
    return [value] + [got[s] for s in (1, 2, 3)]


def gather(panel, own, with_gram):
    inner, pair = join(spread(send_inner, panel), [own, send_y(own, 1)], with_gram)
    outer = spread(send_outer, inner)
    along_y = jnp.concatenate([pair, send_y(pair, 3)])
    return outer, [along_y, send_core(along_y)]


def scatter(parts):
    got = [carry(send_outer, parts[s], s) for s in (1, 2, 3)]
    column, send, *gram = halve(parts[4], carry(send_core, parts[5]), parts[6:])
    column, send, *gram = halve(column, carry(send_y, send, 3), gram)
    along_y = carry(send_y, send, 1)
    row = add_outer(parts[0], got)
    return [row[0], column] + [carry(send_inner, row[s], s) for s in (1, 2, 3)] + [along_y], gram


def hold_kernel(source, target, turned, sems):
    copies = [pltpu.make_async_copy(source.at[k], target.at[k], sems.at[k]) for k in range(3)]
    for copy in copies:
        copy.start()
    for k, copy in enumerate(copies):
        copy.wait()
        turned[k] = target[k].T


def hold(blocks):
    return pl.pallas_call(
        hold_kernel,
        out_shape=[struct(blocks.shape, blocks.dtype)] * 2,
        in_specs=[pl.BlockSpec(memory_space=pl.ANY)],
        out_specs=[VMEM] * 2,
        scratch_shapes=[pltpu.SemaphoreType.DMA((3,))],
        compiler_params=PARAMS,
        cost_estimate=pl.CostEstimate(flops=0, bytes_accessed=6_000_000, transcendentals=0),
        name="hold",
    )(blocks)


def load(panel):
    return pl.pallas_call(
        lambda source, target: target.__setitem__(..., source[...]),
        out_shape=struct(panel.shape, panel.dtype),
        in_specs=[VMEM],
        out_specs=VMEM,
        compiler_params=PARAMS,
        name="load",
    )(panel)


def on_device(block_pairs, live_counts, pair_blocks, start_basis):
    users = 128 * start_basis.shape[2]
    root = float(users) ** 0.5
    pair_blocks, turned = hold(pair_blocks)
    gathered, pair_gathered = gather(start_basis[0], start_basis[0], False)
    parts = first_product(block_pairs, live_counts, pair_blocks, turned, gathered, pair_gathered)
    first, panel, own = finish_first(scatter(parts)[0])
    gathered, pair_gathered = gather(panel, own, True)
    parts = second_product(block_pairs, live_counts, pair_blocks, turned, gathered, pair_gathered)
    parts, (gram,) = scatter(parts)
    first_basis, inverse = factor_first(gram, parts[5], first, root)
    scaled, tiles = finish_second(parts, inverse)
    embedding = factor_second(total_gram(tiles), scaled, root)
    return (first_basis[None], embedding[None])


def solution(mesh):
    mesh = Mesh(mesh.devices.reshape(4, 4, 4, 2), AXES)
    spec = P(AXES, None, None)
    return jax.shard_map(
        on_device, mesh=mesh, in_specs=(spec, P(AXES), spec, spec), out_specs=(spec, spec), check_vma=False
    )
```

```python
import functools

import jax
import jax.numpy as jnp
from jax import lax
from jax.experimental import pallas as pl
from jax.experimental.pallas import tpu as pltpu
from jax.sharding import Mesh
from jax.sharding import PartitionSpec as P

AXES = ("z", "x", "y", "core")
HIGHEST = lax.Precision.HIGHEST
VMEM = pl.BlockSpec(memory_space=pltpu.VMEM)
SMEM = pl.BlockSpec(memory_space=pltpu.SMEM)
PARAMS = pltpu.CompilerParams(vmem_limit_bytes=24 * 1024 * 1024)


def permute(value, target):
    pairs = []
    for device in range(128):
        z, x, y, c = device // 32, device // 8 % 4, device // 2 % 4, device % 2
        tz, tx, ty, tc = target(z, x, y, c)
        pairs.append((device, ((tz % 4) * 4 + tx % 4) * 8 + (ty % 4) * 2 + tc % 2))
    return lax.ppermute(value, AXES, pairs)


def send_inner(value, s):
    return permute(value, lambda z, x, y, c: (z + s, x, y, c) if c == 0 else (z, x + s, y, c))


def send_outer(value, s):
    return permute(value, lambda z, x, y, c: (z, x + s, y, c) if c == 0 else (z + s, x, y, c))


def send_y(value, s):
    return permute(value, lambda z, x, y, c: (z, x, y ^ s if c == 0 else y ^ (4 - s), c))


def send_core(value):
    return permute(value, lambda z, x, y, c: (z, x, y, c + 1))


def struct(shape, dtype):
    return jax.ShapeDtypeStruct(shape, dtype)


def fold(gram):
    return jnp.concatenate([gram[8 * k : 8 * k + 8] for k in range(4)], axis=1)


def unfold(tile):
    return jnp.concatenate([tile[:, 32 * k : 32 * k + 32] for k in range(4)], axis=0)


def split(tile):
    terms = []
    for _ in range(3):
        term = tile.astype(jnp.bfloat16).astype(jnp.float32)
        terms.append(term)
        tile = tile - term
    return jnp.concatenate(terms + [jnp.zeros_like(tile)], axis=0).astype(jnp.bfloat16)


def encode(value):
    top = jnp.max(jnp.abs(value), axis=1, keepdims=True)
    power = jnp.floor(jnp.log2(jnp.maximum(top, 1e-30))) - 13.0
    return jnp.concatenate([value * jnp.exp2(-power), jnp.broadcast_to(power, (32, 128))], axis=1)


def decode(value):
    if value.dtype == jnp.bfloat16:
        return value[:, 0:1024].astype(jnp.float32)
    return value[:, 0:1024] * jnp.exp2(value[:, 1024:1025])


def put(ref, k, value):
    for i in range(2):
        for j in range(8):
            ref[16 * k + 8 * i + j] = value[16 * i : 16 * i + 16, 128 * j : 128 * j + 128]


def take(ref, k):
    rows = [jnp.concatenate([ref[16 * k + 8 * i + j] for j in range(8)], axis=1) for i in range(2)]
    return jnp.concatenate(rows, axis=0)


def take_extra(ref, k):
    return jnp.concatenate([ref[16 * k], ref[16 * k + 1]], axis=0)


def put_extra(ref, k, value):
    ref[16 * k] = value[0:16]
    ref[16 * k + 1] = value[16:32]


def carry(send, value, *args):
    if value.dtype == jnp.bfloat16:
        return send(value, *args)
    return send(value.astype(jnp.float16), *args).astype(jnp.float32)


def merge(terms):
    terms = terms.astype(jnp.float32)
    return terms[0:8] + terms[8:16] + terms[16:24]


def places(pairs, slot):
    first, second = pairs[0, slot, 0], pairs[0, slot, 1]
    row, col = first // 8, second % 8
    dz, dx = (second // 8 // 4 - row // 4) & 3, (second // 8 % 4 - row % 4) & 3
    c = col % 2
    outer, inner = jnp.where(c == 0, dx, dz), jnp.where(c == 0, dz, dx)
    dy = (first % 8 // 2) ^ (col // 2)
    dy = dy ^ (dy >> 1)
    dy = jnp.where(first % 2 == 0, dy, (dy & 1) * 2 + (dy >> 1))
    return outer, inner, (first % 2) ^ c, dy


def load_right(pairs, slot, pair_gathered, rights):
    outer, inner, dc, dy = places(pairs, slot)
    for t in range(2):
        @pl.when(dc == t)
        def _():
            rights[...] = pair_gathered[t][dy]


def load_left(pairs, slot, gathered, lefts):
    outer, inner, dc, dy = places(pairs, slot)
    for t in range(4):
        @pl.when((-outer & 3) == t)
        def _():
            lefts[...] = take(gathered[t], -inner & 3)


def multiply(panel, matrix):
    return jnp.dot(panel[...], matrix, preferred_element_type=jnp.float32)


def store_mirror(pairs, slot, value, outs, half):
    outer, inner, dc, dy = places(pairs, slot)
    value = jnp.where(pairs[0, slot, 0] != pairs[0, slot, 1], value, 0.0)
    lanes = lax.broadcasted_iota(jnp.int32, (32, 128), 1)

    @pl.when(outer == 0)
    def _():
        outs[0][inner] = outs[0][inner] + value

    for t in range(1, 4):
        @pl.when(outer == t)
        def _():
            place = jnp.where(lanes == 8 * slot + inner, 1.0, 0.0)
            if half:
                coded = encode(value)
                put(outs[t], slot, coded[:, 0:1024])
                place = place + jnp.where(lanes == 8 * slot + 4, coded[:, 1024:1152], 0.0)
            else:
                put(outs[t], slot, value.astype(jnp.bfloat16))
            extra = take_extra(outs[t], 3).astype(jnp.float32) + place
            put_extra(outs[t], 3, extra.astype(outs[t].dtype))


def store_direct(pairs, slot, value, outs, results, half):
    outer, inner, dc, dy = places(pairs, slot)
    results[slot] = value
    results[3] = value

    def earlier(before, carry):
        @pl.when(pairs[0, before, 0] == pairs[0, slot, 0])
        def _():
            results[3] = results[3] + results[before]

        return carry

    lax.fori_loop(0, slot, earlier, 0)
    for t in range(2):
        @pl.when(dc == t)
        def _():
            if t and half:
                outs[1][dy] = encode(results[3])
            else:
                outs[t][dy, :, 0:1024] = results[3].astype(outs[t].dtype)


def add_gram(gathered, out, sent):
    gram = merge(take_extra(gathered[0], 4))
    for array in gathered[1:]:
        gram = gram + merge(take_extra(array, 4))
    out[...] = gram
    sent[0, :, 1024:1152] = split(gram)


def clear(outs):
    for out in outs:
        out[...] = jnp.zeros_like(out)


def mirror_kernel(half, pairs, live, blocks, h0, h1, *rest):
    outs, (rights,) = rest[:4], rest[4:]
    clear(outs)

    def advance(slot, carry):
        load_right(pairs, slot, (h0, h1), rights)
        store_mirror(pairs, slot, multiply(rights, blocks[slot]), outs, half)
        return carry

    lax.fori_loop(0, live[0], advance, 0)


def direct_kernel(half, pairs, live, turned, g0, g1, g2, g3, after, *rest):
    outs, (lefts, results) = rest[:-2], rest[-2:]
    clear(outs[:2])
    if not half:
        add_gram((g0, g1, g2, g3), outs[2], outs[1])

    def advance(slot, carry):
        load_left(pairs, slot, (g0, g1, g2, g3), lefts)
        store_direct(pairs, slot, multiply(lefts, turned[slot]), outs, results, half)
        return carry

    lax.fori_loop(0, live[0], advance, 0)


PANEL = pltpu.VMEM((32, 1024), jnp.bfloat16)
RESULTS = pltpu.VMEM((4, 32, 1024), jnp.float32)


def product_call(kernel, outs, scratch, name, pairs, live, *arrays):
    return pl.pallas_call(
        kernel,
        out_shape=outs,
        in_specs=[SMEM, SMEM] + [VMEM] * len(arrays),
        out_specs=[VMEM] * len(outs),
        scratch_shapes=scratch,
        compiler_params=PARAMS,
        name=name,
    )(pairs, live, *arrays)


def product(pairs, live, blocks, turned, gathered, pair_gathered, half):
    f32 = jnp.float32
    sent = f32 if half else jnp.bfloat16
    outs = [struct((4, 32, 1024), f32)] + [struct((50, 16, 128), sent)] * 3
    kernel = functools.partial(mirror_kernel, half)
    rows = product_call(kernel, outs, [PANEL], "mirror", pairs, live, blocks, *pair_gathered)
    outs = [struct((4, 32, 1024), f32), struct((4, 32, 1152), sent)]
    outs += [] if half else [struct((8, 128), f32)]
    kernel = functools.partial(direct_kernel, half)
    arrays = (turned, *gathered, rows[0])
    return rows + product_call(kernel, outs, [PANEL, RESULTS], "direct", pairs, live, *arrays)


def join_kernel(with_gram, *refs):
    parts, pair, joined, joined_pair = refs[:4], refs[4:6], refs[6], refs[7]
    for k, part in enumerate(parts):
        put(joined, k, part[:, 0:1024])
    if with_gram:
        gram = merge(parts[0][:, 1024:1152])
        for part in parts[1:]:
            gram = gram + merge(part[:, 1024:1152])
        put_extra(joined, 4, split(gram))
    else:
        put_extra(joined, 4, jnp.zeros((32, 128), jnp.bfloat16))
    for k, part in enumerate(pair):
        joined_pair[k] = part[...]


def join(parts, pair, with_gram):
    shapes = [(66, 16, 128), (2,) + pair[0].shape]
    return pl.pallas_call(
        functools.partial(join_kernel, with_gram),
        out_shape=[struct(shape, jnp.bfloat16) for shape in shapes],
        in_specs=[VMEM] * 6,
        out_specs=[VMEM] * 2,
        compiler_params=PARAMS,
        name="join",
    )(*parts, *pair)


def halve_kernel(with_gram, own, received, *rest):
    outs = rest[with_gram:]
    keep, send = outs[:2]
    half = keep.shape[0]
    for k in range(2 * half):
        value = own[k] + decode(received[k])
        if k < half:
            keep[k] = value
        elif not with_gram:
            send[k - half] = encode(value)
        else:
            send[k - half, :, 0:1024] = value.astype(send.dtype)
    if with_gram:
        gram = rest[0][...] + merge(received[0, :, 1024:1152])
        outs[2][...] = gram
        for k in range(half):
            send[k, :, 1024:1152] = split(gram)


def halve(own, received, gram):
    f32 = jnp.float32
    half = own.shape[0] // 2
    outs = [struct((half, 32, 1024), f32), struct((half,) + received.shape[1:], received.dtype)]
    outs += [struct((8, 128), f32)] * len(gram)
    return pl.pallas_call(
        functools.partial(halve_kernel, len(gram)),
        out_shape=outs,
        in_specs=[VMEM] * (2 + len(gram)),
        out_specs=[VMEM] * len(outs),
        compiler_params=PARAMS,
        name="halve",
    )(own, received, *gram)


def row_kernel(half, own, *refs):
    received, outs, (weights, total) = refs[:3], refs[3:7], refs[7:]
    entries = [(array, k) for array in received for k in range(3)]
    extras = [take_extra(array, 3).astype(jnp.float32) for array in received]
    for e, (array, k) in enumerate(entries):
        extra = extras[e // 3]
        scale = jnp.exp2(extra[:, 8 * k + 4 : 8 * k + 5]) if half else 1.0
        for s in range(4):
            weights[4 * e + s] = jnp.broadcast_to(extra[:, 8 * k + s : 8 * k + s + 1] * scale, (32, 128))
    for i in range(2):
        rows = slice(16 * i, 16 * i + 16)
        for j in range(8):
            columns = slice(128 * j, 128 * j + 128)
            sums = [own[s, rows, columns] for s in range(4)]
            for e, (array, k) in enumerate(entries):
                value = array[16 * k + 8 * i + j].astype(jnp.float32)
                for s in range(4):
                    sums[s] = sums[s] + value * weights[4 * e + s, rows]
            for s in range(4):
                total[s, rows, columns] = sums[s]
    outs[0][...] = total[0]
    for s in range(1, 4):
        outs[s][...] = encode(total[s]) if half else total[s].astype(outs[s].dtype)


def add_outer(own, received):
    half = received[0].dtype == jnp.float32
    sent = struct((32, 1152), jnp.float32) if half else struct((32, 1024), jnp.bfloat16)
    return pl.pallas_call(
        functools.partial(row_kernel, half),
        out_shape=[struct((32, 1024), jnp.float32)] + [sent] * 3,
        in_specs=[VMEM] * 4,
        out_specs=[VMEM] * 4,
        scratch_shapes=[pltpu.VMEM((36, 32, 128), jnp.float32), pltpu.VMEM((4, 32, 1024), jnp.float32)],
        compiler_params=PARAMS,
        name="add_outer",
    )(own, *received)


def add_parts(parts):
    value = parts[0][...] + parts[1][0]
    for part in parts[2:5]:
        value = value + decode(part[...])
    return value + decode(parts[5][0])


def first_kernel(*refs):
    parts, (first, panel, own) = refs[:6], refs[6:]
    value = add_parts(parts)
    first[...] = value
    rounded = value.astype(jnp.bfloat16)
    panel[:, 0:1024] = rounded
    own[...] = rounded
    panel[:, 1024:1152] = split(
        fold(
            lax.dot_general(
                rounded, rounded, (((1,), (1,)), ((), ())), preferred_element_type=jnp.float32
            )
        )
    )


def finish_first(parts):
    return pl.pallas_call(
        first_kernel,
        out_shape=[
            struct((32, 1024), jnp.float32),
            struct((32, 1152), jnp.bfloat16),
            struct((32, 1024), jnp.bfloat16),
        ],
        in_specs=[VMEM] * 6,
        out_specs=[VMEM] * 3,
        compiler_params=PARAMS,
        name="finish_first",
    )(*parts)


def second_kernel(*refs):
    parts, inverse, (scaled, gram) = refs[:6], refs[6], refs[7:]
    value = add_parts(parts)
    value = jnp.dot(inverse[...], value, precision=HIGHEST, preferred_element_type=jnp.float32)
    scaled[...] = value
    tile = fold(
        lax.dot_general(
            value, value, (((1,), (1,)), ((), ())), precision=HIGHEST, preferred_element_type=jnp.float32
        )
    )
    gram[...] = tile


def finish_second(parts, inverse):
    return pl.pallas_call(
        second_kernel,
        out_shape=[struct((32, 1024), jnp.float32), struct((8, 128), jnp.float32)],
        in_specs=[VMEM] * 7,
        out_specs=[VMEM] * 2,
        compiler_params=PARAMS,
        name="finish_second",
    )(*parts, inverse)


def total_kernel(own, other, out):
    total = own[...] + other[...]
    for k in range(64):
        out[k] = total


def total_gram(tile):
    tiles = pl.pallas_call(
        total_kernel,
        out_shape=struct((64, 8, 128), jnp.float32),
        in_specs=[VMEM] * 2,
        out_specs=VMEM,
        compiler_params=PARAMS,
        name="total_gram",
    )(tile, send_core(tile))
    return lax.all_to_all(tiles, ("z", "x", "y"), 0, 0, tiled=True)


def lower_inverse(gram):
    rows = lax.broadcasted_iota(jnp.int32, (32, 128), 0)
    lanes = lax.broadcasted_iota(jnp.int32, (32, 128), 1)
    wide = jnp.concatenate([gram, jnp.zeros((32, 96), jnp.float32)], axis=1)
    wide = jnp.where(lanes == rows + 32, 1.0, wide)
    parts = [wide[8 * k : 8 * k + 8] for k in range(4)]
    inside = rows[0:8]
    for step in range(4):
        columns = [
            [jnp.broadcast_to(part[:, k : k + 1], (8, 128)) for k in range(8 * step, 8 * step + 8)]
            for part in parts
        ]
        pivot = parts[step]
        schur = {(i, j): columns[step][j][i : i + 1] for i in range(8) for j in range(i + 1)}
        lines = [pivot[i : i + 1] for i in range(8)]
        factors, inverses = {}, []
        for j in range(8):
            inverses.append(1.0 / schur[j, j])
            for i in range(j + 1, 8):
                factors[i, j] = schur[i, j] * inverses[j]
            for i in range(j + 1, 8):
                for t in range(j + 1, i + 1):
                    schur[i, t] = schur[i, t] - factors[i, j] * schur[t, j]
                lines[i] = lines[i] - factors[i, j] * lines[j]
        for i in range(1, 8):
            pivot = jnp.where(inside == i, lines[i], pivot)
        parts[step] = pivot
        solved = [None] * 8
        for j in reversed(range(8)):
            value = lines[j] * inverses[j]
            for i in range(j + 1, 8):
                value = value - factors[i, j] * solved[i]
            solved[j] = value
        for later in range(step + 1, 4):
            for j in range(8):
                parts[later] = parts[later] - columns[later][j] * solved[j]
    wide = jnp.concatenate(parts, axis=0)
    diagonal = jnp.sum(jnp.where(lanes == rows, wide, 0.0), axis=1, keepdims=True)
    wide = wide / jnp.sqrt(diagonal)
    return wide[:, 32:64]


def factor_kernel(root, gram, panel, *outs):
    tile = gram[0]
    for k in range(1, 64):
        tile = tile + gram[k]
    inverse = lower_inverse(unfold(tile))
    outs[0][...] = (
        jnp.dot(inverse, panel[...], precision=HIGHEST, preferred_element_type=jnp.float32) * root
    )


def factor_first_kernel(root, gram, received, panel, basis, inverse):
    inverse[...] = lower_inverse(unfold(gram[...] + merge(received[0, :, 1024:1152])))
    basis[...] = (
        jnp.dot(inverse[...], panel[...], precision=HIGHEST, preferred_element_type=jnp.float32) * root
    )


def factor_first(gram, received, first, root):
    return pl.pallas_call(
        functools.partial(factor_first_kernel, root),
        out_shape=[struct((32, 1024), jnp.float32), struct((32, 32), jnp.float32)],
        in_specs=[VMEM] * 3,
        out_specs=[VMEM] * 2,
        compiler_params=PARAMS,
        cost_estimate=pl.CostEstimate(flops=1_000_000, bytes_accessed=10_000_000, transcendentals=0),
        name="factor_first",
    )(gram, received, first)


def factor_second(gram, scaled, root):
    return pl.pallas_call(
        functools.partial(factor_kernel, root),
        out_shape=struct((32, 1024), jnp.float32),
        in_specs=[VMEM] * 2,
        out_specs=VMEM,
        compiler_params=PARAMS,
        name="factor_second",
    )(gram, scaled)


SHIFTS = (1, 3, 2)


def spread(send, value):
    got = {s: send(value, s) for s in SHIFTS}
    return [value] + [got[s] for s in (1, 2, 3)]


def gather(panel, own, with_gram):
    inner, pair = join(spread(send_inner, panel), [own, send_y(own, 1)], with_gram)
    outer = spread(send_outer, inner)
    along_y = jnp.concatenate([pair, send_y(pair, 3)])
    return outer, [along_y, send_core(along_y)]


def scatter(parts):
    got = [carry(send_outer, parts[s], s) for s in (1, 2, 3)]
    column, send, *gram = halve(parts[4], carry(send_core, parts[5]), parts[6:])
    column, send, *gram = halve(column, carry(send_y, send, 3), gram)
    along_y = carry(send_y, send, 1)
    row = add_outer(parts[0], got)
    return [row[0], column] + [carry(send_inner, row[s], s) for s in (1, 2, 3)] + [along_y], gram


def turn_kernel(source, turned):
    for k in range(3):
        turned[k] = source[k].T


def turn(blocks):
    return pl.pallas_call(
        turn_kernel,
        out_shape=struct(blocks.shape, blocks.dtype),
        in_specs=[VMEM],
        out_specs=VMEM,
        compiler_params=PARAMS,
        cost_estimate=pl.CostEstimate(flops=0, bytes_accessed=6_000_000, transcendentals=0),
        name="turn",
    )(blocks)


def on_device(block_pairs, live_counts, pair_blocks, start_basis):
    users = 128 * start_basis.shape[2]
    root = float(users) ** 0.5
    turned = turn(pair_blocks)
    gathered, pair_gathered = gather(start_basis[0], start_basis[0], False)
    parts = product(block_pairs, live_counts, pair_blocks, turned, gathered, pair_gathered, True)
    first, panel, own = finish_first(scatter(parts)[0])
    gathered, pair_gathered = gather(panel, own, True)
    parts = product(block_pairs, live_counts, pair_blocks, turned, gathered, pair_gathered, False)
    parts, (gram,) = scatter(parts)
    first_basis, inverse = factor_first(gram, parts[5], first, root)
    scaled, tiles = finish_second(parts, inverse)
    embedding = factor_second(total_gram(tiles), scaled, root)
    return (first_basis[None], embedding[None])


def solution(mesh):
    mesh = Mesh(mesh.devices.reshape(4, 4, 4, 2), AXES)
    spec = P(AXES, None, None)
    return jax.shard_map(
        on_device, mesh=mesh, in_specs=(spec, P(AXES), spec, spec), out_specs=(spec, spec), check_vma=False
    )
```

```python
import functools

import jax
import jax.numpy as jnp
from jax import lax
from jax.experimental import pallas as pl
from jax.experimental.pallas import tpu as pltpu
from jax.sharding import Mesh
from jax.sharding import PartitionSpec as P

AXES = ("z", "x", "y", "core")
HIGHEST = lax.Precision.HIGHEST
VMEM = pl.BlockSpec(memory_space=pltpu.VMEM)
SMEM = pl.BlockSpec(memory_space=pltpu.SMEM)
PARAMS = pltpu.CompilerParams(vmem_limit_bytes=24 * 1024 * 1024)


def permute(value, target):
    pairs = []
    for device in range(128):
        z, x, y, c = device // 32, device // 8 % 4, device // 2 % 4, device % 2
        tz, tx, ty, tc = target(z, x, y, c)
        pairs.append((device, ((tz % 4) * 4 + tx % 4) * 8 + (ty % 4) * 2 + tc % 2))
    return lax.ppermute(value, AXES, pairs)


def send_inner(value, s):
    return permute(value, lambda z, x, y, c: (z + s, x, y, c) if c == 0 else (z, x + s, y, c))


def send_outer(value, s):
    return permute(value, lambda z, x, y, c: (z, x + s, y, c) if c == 0 else (z + s, x, y, c))


def send_y(value, s):
    return permute(value, lambda z, x, y, c: (z, x, y ^ s if c == 0 else y ^ (4 - s), c))


def send_core(value):
    return permute(value, lambda z, x, y, c: (z, x, y, c + 1))


def struct(shape, dtype):
    return jax.ShapeDtypeStruct(shape, dtype)


def fold(gram):
    return jnp.concatenate([gram[8 * k : 8 * k + 8] for k in range(4)], axis=1)


def unfold(tile):
    return jnp.concatenate([tile[:, 32 * k : 32 * k + 32] for k in range(4)], axis=0)


def split(tile):
    terms = []
    for _ in range(3):
        term = tile.astype(jnp.bfloat16).astype(jnp.float32)
        terms.append(term)
        tile = tile - term
    return jnp.concatenate(terms + [jnp.zeros_like(tile)], axis=0).astype(jnp.bfloat16)


def encode(value):
    top = jnp.max(jnp.abs(value), axis=1, keepdims=True)
    power = jnp.floor(jnp.log2(jnp.maximum(top, 1e-30))) - 13.0
    return jnp.concatenate([value * jnp.exp2(-power), jnp.broadcast_to(power, (32, 128))], axis=1)


def decode(value):
    if value.dtype == jnp.bfloat16:
        return value[:, 0:1024].astype(jnp.float32)
    return value[:, 0:1024] * jnp.exp2(value[:, 1024:1025])


def put(ref, k, value):
    for i in range(2):
        for j in range(8):
            ref[16 * k + 8 * i + j] = value[16 * i : 16 * i + 16, 128 * j : 128 * j + 128]


def take(ref, k):
    rows = [jnp.concatenate([ref[16 * k + 8 * i + j] for j in range(8)], axis=1) for i in range(2)]
    return jnp.concatenate(rows, axis=0)


def take_extra(ref, k):
    return jnp.concatenate([ref[16 * k], ref[16 * k + 1]], axis=0)


def put_extra(ref, k, value):
    ref[16 * k] = value[0:16]
    ref[16 * k + 1] = value[16:32]


def carry(send, value, *args):
    if value.dtype == jnp.bfloat16:
        return send(value, *args)
    return send(value.astype(jnp.float16), *args).astype(jnp.float32)


def merge(terms):
    terms = terms.astype(jnp.float32)
    return terms[0:8] + terms[8:16] + terms[16:24]


def places(pairs, slot):
    first, second = pairs[0, slot, 0], pairs[0, slot, 1]
    row, col = first // 8, second % 8
    dz, dx = (second // 8 // 4 - row // 4) & 3, (second // 8 % 4 - row % 4) & 3
    c = col % 2
    outer, inner = jnp.where(c == 0, dx, dz), jnp.where(c == 0, dz, dx)
    dy = (first % 8 // 2) ^ (col // 2)
    dy = dy ^ (dy >> 1)
    dy = jnp.where(first % 2 == 0, dy, (dy & 1) * 2 + (dy >> 1))
    return outer, inner, (first % 2) ^ c, dy


def load_right(pairs, slot, pair_gathered, rights):
    outer, inner, dc, dy = places(pairs, slot)
    for t in range(2):
        @pl.when(dc == t)
        def _():
            rights[...] = pair_gathered[t][dy]


def load_left(pairs, slot, gathered, lefts):
    outer, inner, dc, dy = places(pairs, slot)
    for t in range(4):
        @pl.when((-outer & 3) == t)
        def _():
            lefts[...] = take(gathered[t], -inner & 3)


def multiply(panel, matrix):
    return jnp.dot(panel[...], matrix, preferred_element_type=jnp.float32)


def store_mirror(pairs, slot, value, outs, half):
    outer, inner, dc, dy = places(pairs, slot)
    value = jnp.where(pairs[0, slot, 0] != pairs[0, slot, 1], value, 0.0)
    lanes = lax.broadcasted_iota(jnp.int32, (32, 128), 1)

    @pl.when(outer == 0)
    def _():
        outs[0][inner] = outs[0][inner] + value

    for t in range(1, 4):
        @pl.when(outer == t)
        def _():
            place = jnp.where(lanes == 8 * slot + inner, 1.0, 0.0)
            if half:
                coded = encode(value)
                put(outs[t], slot, coded[:, 0:1024])
                place = place + jnp.where(lanes == 8 * slot + 4, coded[:, 1024:1152], 0.0)
            else:
                put(outs[t], slot, value.astype(jnp.bfloat16))
            extra = take_extra(outs[t], 3).astype(jnp.float32) + place
            put_extra(outs[t], 3, extra.astype(outs[t].dtype))


def store_direct(pairs, slot, value, outs, results, half):
    outer, inner, dc, dy = places(pairs, slot)
    results[slot] = value
    results[3] = value

    def earlier(before, carry):
        @pl.when(pairs[0, before, 0] == pairs[0, slot, 0])
        def _():
            results[3] = results[3] + results[before]

        return carry

    lax.fori_loop(0, slot, earlier, 0)
    for t in range(2):
        @pl.when(dc == t)
        def _():
            if t and half:
                outs[1][dy] = encode(results[3])
            else:
                outs[t][dy, :, 0:1024] = results[3].astype(outs[t].dtype)


def add_gram(gathered, out, sent):
    gram = merge(take_extra(gathered[0], 4))
    for array in gathered[1:]:
        gram = gram + merge(take_extra(array, 4))
    out[...] = gram
    sent[0, :, 1024:1152] = split(gram)


def clear(outs):
    for out in outs:
        out[...] = jnp.zeros_like(out)


def mirror_kernel(half, pairs, live, blocks, h0, h1, *rest):
    outs, (rights,) = rest[:4], rest[4:]
    clear(outs)

    def advance(slot, carry):
        load_right(pairs, slot, (h0, h1), rights)
        store_mirror(pairs, slot, multiply(rights, blocks[slot]), outs, half)
        return carry

    lax.fori_loop(0, live[0], advance, 0)


def direct_kernel(half, pairs, live, turned, g0, g1, g2, g3, after, *rest):
    outs, (lefts, results) = rest[:-2], rest[-2:]
    clear(outs[:2])
    if not half:
        add_gram((g0, g1, g2, g3), outs[2], outs[1])

    def advance(slot, carry):
        load_left(pairs, slot, (g0, g1, g2, g3), lefts)
        store_direct(pairs, slot, multiply(lefts, turned[slot]), outs, results, half)
        return carry

    lax.fori_loop(0, live[0], advance, 0)


PANEL = pltpu.VMEM((32, 1024), jnp.bfloat16)
RESULTS = pltpu.VMEM((4, 32, 1024), jnp.float32)


def product_call(kernel, outs, scratch, name, pairs, live, *arrays):
    return pl.pallas_call(
        kernel,
        out_shape=outs,
        in_specs=[SMEM, SMEM] + [VMEM] * len(arrays),
        out_specs=[VMEM] * len(outs),
        scratch_shapes=scratch,
        compiler_params=PARAMS,
        name=name,
    )(pairs, live, *arrays)


def product(pairs, live, blocks, turned, gathered, pair_gathered, half):
    f32 = jnp.float32
    sent = f32 if half else jnp.bfloat16
    outs = [struct((4, 32, 1024), f32)] + [struct((50, 16, 128), sent)] * 3
    kernel = functools.partial(mirror_kernel, half)
    rows = product_call(kernel, outs, [PANEL], "mirror", pairs, live, blocks, *pair_gathered)
    outs = [struct((4, 32, 1024), f32), struct((4, 32, 1152), sent)]
    outs += [] if half else [struct((8, 128), f32)]
    kernel = functools.partial(direct_kernel, half)
    arrays = (turned, *gathered, rows[0])
    return rows + product_call(kernel, outs, [PANEL, RESULTS], "direct", pairs, live, *arrays)


def join_kernel(with_gram, *refs):
    parts, pair, joined, joined_pair = refs[:4], refs[4:6], refs[6], refs[7]
    for k, part in enumerate(parts):
        put(joined, k, part[:, 0:1024])
    if with_gram:
        gram = merge(parts[0][:, 1024:1152])
        for part in parts[1:]:
            gram = gram + merge(part[:, 1024:1152])
        put_extra(joined, 4, split(gram))
    else:
        put_extra(joined, 4, jnp.zeros((32, 128), jnp.bfloat16))
    for k, part in enumerate(pair):
        joined_pair[k] = part[...]


def join(parts, pair, with_gram):
    shapes = [(66, 16, 128), (2,) + pair[0].shape]
    return pl.pallas_call(
        functools.partial(join_kernel, with_gram),
        out_shape=[struct(shape, jnp.bfloat16) for shape in shapes],
        in_specs=[VMEM] * 6,
        out_specs=[VMEM] * 2,
        compiler_params=PARAMS,
        name="join",
    )(*parts, *pair)


def halve_kernel(with_gram, own, received, *rest):
    outs = rest[with_gram:]
    keep, send = outs[:2]
    half = keep.shape[0]
    for k in range(2 * half):
        value = own[k] + decode(received[k])
        if k < half:
            keep[k] = value
        elif not with_gram:
            send[k - half] = encode(value)
        else:
            send[k - half, :, 0:1024] = value.astype(send.dtype)
    if with_gram:
        gram = rest[0][...] + merge(received[0, :, 1024:1152])
        outs[2][...] = gram
        for k in range(half):
            send[k, :, 1024:1152] = split(gram)


def halve(own, received, gram):
    f32 = jnp.float32
    half = own.shape[0] // 2
    outs = [struct((half, 32, 1024), f32), struct((half,) + received.shape[1:], received.dtype)]
    outs += [struct((8, 128), f32)] * len(gram)
    return pl.pallas_call(
        functools.partial(halve_kernel, len(gram)),
        out_shape=outs,
        in_specs=[VMEM] * (2 + len(gram)),
        out_specs=[VMEM] * len(outs),
        compiler_params=PARAMS,
        name="halve",
    )(own, received, *gram)


def row_kernel(half, own, *refs):
    received, outs, (weights, total) = refs[:3], refs[3:7], refs[7:]
    entries = [(array, k) for array in received for k in range(3)]
    extras = [take_extra(array, 3).astype(jnp.float32) for array in received]
    powers = [jnp.exp2(extra) for extra in extras]
    for e, (array, k) in enumerate(entries):
        extra = extras[e // 3]
        scale = powers[e // 3][:, 8 * k + 4 : 8 * k + 5] if half else 1.0
        for s in range(4):
            weights[4 * e + s] = jnp.broadcast_to(extra[:, 8 * k + s : 8 * k + s + 1] * scale, (32, 128))
    for i in range(2):
        rows = slice(16 * i, 16 * i + 16)
        for j in range(8):
            columns = slice(128 * j, 128 * j + 128)
            sums = [own[s, rows, columns] for s in range(4)]
            for e, (array, k) in enumerate(entries):
                value = array[16 * k + 8 * i + j].astype(jnp.float32)
                for s in range(4):
                    sums[s] = sums[s] + value * weights[4 * e + s, rows]
            for s in range(4):
                total[s, rows, columns] = sums[s]
    outs[0][...] = total[0]
    for s in range(1, 4):
        outs[s][...] = encode(total[s]) if half else total[s].astype(outs[s].dtype)


def add_outer(own, received):
    half = received[0].dtype == jnp.float32
    sent = struct((32, 1152), jnp.float32) if half else struct((32, 1024), jnp.bfloat16)
    return pl.pallas_call(
        functools.partial(row_kernel, half),
        out_shape=[struct((32, 1024), jnp.float32)] + [sent] * 3,
        in_specs=[VMEM] * 4,
        out_specs=[VMEM] * 4,
        scratch_shapes=[pltpu.VMEM((36, 32, 128), jnp.float32), pltpu.VMEM((4, 32, 1024), jnp.float32)],
        compiler_params=PARAMS,
        name="add_outer",
    )(own, *received)


def add_parts(parts):
    value = parts[0][...] + parts[1][0]
    for part in parts[2:5]:
        value = value + decode(part[...])
    return value + decode(parts[5][0])


def first_kernel(*refs):
    parts, (first, panel, own) = refs[:6], refs[6:]
    value = add_parts(parts)
    first[...] = value
    rounded = value.astype(jnp.bfloat16)
    panel[:, 0:1024] = rounded
    own[...] = rounded
    panel[:, 1024:1152] = split(
        fold(
            lax.dot_general(
                rounded, rounded, (((1,), (1,)), ((), ())), preferred_element_type=jnp.float32
            )
        )
    )


def finish_first(parts):
    return pl.pallas_call(
        first_kernel,
        out_shape=[
            struct((32, 1024), jnp.float32),
            struct((32, 1152), jnp.bfloat16),
            struct((32, 1024), jnp.bfloat16),
        ],
        in_specs=[VMEM] * 6,
        out_specs=[VMEM] * 3,
        compiler_params=PARAMS,
        name="finish_first",
    )(*parts)


def second_kernel(*refs):
    parts, inverse, (scaled, gram) = refs[:6], refs[6], refs[7:]
    value = add_parts(parts)
    value = jnp.dot(inverse[...], value, precision=HIGHEST, preferred_element_type=jnp.float32)
    scaled[...] = value
    tile = fold(
        lax.dot_general(
            value, value, (((1,), (1,)), ((), ())), precision=HIGHEST, preferred_element_type=jnp.float32
        )
    )
    gram[...] = tile


def finish_second(parts, inverse):
    return pl.pallas_call(
        second_kernel,
        out_shape=[struct((32, 1024), jnp.float32), struct((8, 128), jnp.float32)],
        in_specs=[VMEM] * 7,
        out_specs=[VMEM] * 2,
        compiler_params=PARAMS,
        name="finish_second",
    )(*parts, inverse)


def total_kernel(own, other, after, out):
    total = own[...] + other[...]
    for k in range(64):
        out[k] = total


def total_gram(tile, after):
    tiles = pl.pallas_call(
        total_kernel,
        out_shape=struct((64, 8, 128), jnp.float32),
        in_specs=[VMEM] * 2 + [pl.BlockSpec(memory_space=pl.ANY)],
        out_specs=VMEM,
        compiler_params=PARAMS,
        name="total_gram",
    )(tile, send_core(tile), after)
    return lax.all_to_all(tiles, ("z", "x", "y"), 0, 0, tiled=True)


def lower_inverse(gram):
    rows = lax.broadcasted_iota(jnp.int32, (32, 128), 0)
    lanes = lax.broadcasted_iota(jnp.int32, (32, 128), 1)
    wide = jnp.concatenate([gram, jnp.zeros((32, 96), jnp.float32)], axis=1)
    wide = jnp.where(lanes == rows + 32, 1.0, wide)
    parts = [wide[8 * k : 8 * k + 8] for k in range(4)]
    inside = rows[0:8]
    for step in range(4):
        columns = [
            [jnp.broadcast_to(part[:, k : k + 1], (8, 128)) for k in range(8 * step, 8 * step + 8)]
            for part in parts
        ]
        pivot = parts[step]
        schur = {(i, j): columns[step][j][i : i + 1] for i in range(8) for j in range(i + 1)}
        lines = [pivot[i : i + 1] for i in range(8)]
        factors, inverses = {}, []
        for j in range(8):
            inverses.append(1.0 / schur[j, j])
            for i in range(j + 1, 8):
                factors[i, j] = schur[i, j] * inverses[j]
            for i in range(j + 1, 8):
                for t in range(j + 1, i + 1):
                    schur[i, t] = schur[i, t] - factors[i, j] * schur[t, j]
                lines[i] = lines[i] - factors[i, j] * lines[j]
        for i in range(1, 8):
            pivot = jnp.where(inside == i, lines[i], pivot)
        parts[step] = pivot
        solved = [None] * 8
        for j in reversed(range(8)):
            value = lines[j] * inverses[j]
            for i in range(j + 1, 8):
                value = value - factors[i, j] * solved[i]
            solved[j] = value
        for later in range(step + 1, 4):
            for j in range(8):
                parts[later] = parts[later] - columns[later][j] * solved[j]
    wide = jnp.concatenate(parts, axis=0)
    diagonal = jnp.sum(jnp.where(lanes == rows, wide, 0.0), axis=1, keepdims=True)
    wide = wide / jnp.sqrt(diagonal)
    return wide[:, 32:64]


def factor_kernel(root, gram, panel, *outs):
    tile = gram[0]
    for k in range(1, 64):
        tile = tile + gram[k]
    inverse = lower_inverse(unfold(tile))
    outs[0][...] = (
        jnp.dot(inverse, panel[...], precision=HIGHEST, preferred_element_type=jnp.float32) * root
    )


def invert_kernel(gram, received, inverse):
    inverse[...] = lower_inverse(unfold(gram[...] + merge(received[0, :, 1024:1152])))


def invert_first(gram, received):
    return pl.pallas_call(
        invert_kernel,
        out_shape=struct((32, 32), jnp.float32),
        in_specs=[VMEM] * 2,
        out_specs=VMEM,
        compiler_params=PARAMS,
        name="invert_first",
    )(gram, received)


def basis_kernel(root, inverse, first, after, basis, done):
    basis[...] = (
        jnp.dot(inverse[...], first[...], precision=HIGHEST, preferred_element_type=jnp.float32) * root
    )
    done[...] = jnp.zeros_like(done)


def apply_first(inverse, first, after, root):
    return pl.pallas_call(
        functools.partial(basis_kernel, root),
        out_shape=[struct((32, 1024), jnp.float32), struct((8, 128), jnp.float32)],
        in_specs=[VMEM] * 2 + [pl.BlockSpec(memory_space=pl.ANY)],
        out_specs=[VMEM] * 2,
        compiler_params=PARAMS,
        name="apply_first",
    )(inverse, first, after)


def factor_second(gram, scaled, root):
    return pl.pallas_call(
        functools.partial(factor_kernel, root),
        out_shape=struct((32, 1024), jnp.float32),
        in_specs=[VMEM] * 2,
        out_specs=VMEM,
        compiler_params=PARAMS,
        name="factor_second",
    )(gram, scaled)


SHIFTS = (1, 3, 2)


def spread(send, value):
    got = {s: send(value, s) for s in SHIFTS}
    return [value] + [got[s] for s in (1, 2, 3)]


def gather(panel, own, with_gram):
    inner, pair = join(spread(send_inner, panel), [own, send_y(own, 1)], with_gram)
    outer = spread(send_outer, inner)
    along_y = jnp.concatenate([pair, send_y(pair, 3)])
    return outer, [along_y, send_core(along_y)]


def scatter(parts):
    got = [carry(send_outer, parts[s], s) for s in (1, 2, 3)]
    column, send, *gram = halve(parts[4], carry(send_core, parts[5]), parts[6:])
    column, send, *gram = halve(column, carry(send_y, send, 3), gram)
    along_y = carry(send_y, send, 1)
    row = add_outer(parts[0], got)
    return [row[0], column] + [carry(send_inner, row[s], s) for s in (1, 2, 3)] + [along_y], gram


def turn_kernel(source, turned):
    for k in range(3):
        turned[k] = source[k].T


def turn(blocks):
    return pl.pallas_call(
        turn_kernel,
        out_shape=struct(blocks.shape, blocks.dtype),
        in_specs=[VMEM],
        out_specs=VMEM,
        compiler_params=PARAMS,
        cost_estimate=pl.CostEstimate(flops=0, bytes_accessed=6_000_000, transcendentals=0),
        name="turn",
    )(blocks)


def on_device(block_pairs, live_counts, pair_blocks, start_basis):
    users = 128 * start_basis.shape[2]
    root = float(users) ** 0.5
    turned = turn(pair_blocks)
    gathered, pair_gathered = gather(start_basis[0], start_basis[0], False)
    parts = product(block_pairs, live_counts, pair_blocks, turned, gathered, pair_gathered, True)
    first, panel, own = finish_first(scatter(parts)[0])
    gathered, pair_gathered = gather(panel, own, True)
    parts = product(block_pairs, live_counts, pair_blocks, turned, gathered, pair_gathered, False)
    parts, (gram,) = scatter(parts)
    inverse = invert_first(gram, parts[5])
    scaled, tile = finish_second(parts, inverse)
    first_basis, done = apply_first(inverse, first, tile, root)
    embedding = factor_second(total_gram(tile, done), scaled, root)
    return (first_basis[None], embedding[None])


def solution(mesh):
    mesh = Mesh(mesh.devices.reshape(4, 4, 4, 2), AXES)
    spec = P(AXES, None, None)
    return jax.shard_map(
        on_device, mesh=mesh, in_specs=(spec, P(AXES), spec, spec), out_specs=(spec, spec), check_vma=False
    )
```

```python
import functools

import jax
import jax.numpy as jnp
from jax import lax
from jax.experimental import pallas as pl
from jax.experimental.pallas import tpu as pltpu
from jax.sharding import Mesh
from jax.sharding import PartitionSpec as P

AXES = ("z", "x", "y", "core")
HIGHEST = lax.Precision.HIGHEST
VMEM = pl.BlockSpec(memory_space=pltpu.VMEM)
SMEM = pl.BlockSpec(memory_space=pltpu.SMEM)
PARAMS = pltpu.CompilerParams(vmem_limit_bytes=24 * 1024 * 1024)


def permute(value, target):
    pairs = []
    for device in range(128):
        z, x, y, c = device // 32, device // 8 % 4, device // 2 % 4, device % 2
        tz, tx, ty, tc = target(z, x, y, c)
        pairs.append((device, ((tz % 4) * 4 + tx % 4) * 8 + (ty % 4) * 2 + tc % 2))
    return lax.ppermute(value, AXES, pairs)


def send_inner(value, s):
    return permute(value, lambda z, x, y, c: (z + s, x, y, c) if c == 0 else (z, x + s, y, c))


def send_outer(value, s):
    return permute(value, lambda z, x, y, c: (z, x + s, y, c) if c == 0 else (z + s, x, y, c))


def send_y(value, s):
    return permute(value, lambda z, x, y, c: (z, x, y ^ s if c == 0 else y ^ (4 - s), c))


def send_core(value):
    return permute(value, lambda z, x, y, c: (z, x, y, c + 1))


def struct(shape, dtype):
    return jax.ShapeDtypeStruct(shape, dtype)


def fold(gram):
    return jnp.concatenate([gram[8 * k : 8 * k + 8] for k in range(4)], axis=1)


def unfold(tile):
    return jnp.concatenate([tile[:, 32 * k : 32 * k + 32] for k in range(4)], axis=0)


def split(tile):
    terms = []
    for _ in range(3):
        term = tile.astype(jnp.bfloat16).astype(jnp.float32)
        terms.append(term)
        tile = tile - term
    return jnp.concatenate(terms + [jnp.zeros_like(tile)], axis=0).astype(jnp.bfloat16)


def encode(value):
    top = jnp.max(jnp.abs(value), axis=1, keepdims=True)
    power = jnp.floor(jnp.log2(jnp.maximum(top, 1e-30))) - 13.0
    return jnp.concatenate([value * jnp.exp2(-power), jnp.broadcast_to(power, (32, 128))], axis=1)


def decode(value):
    if value.dtype == jnp.bfloat16:
        return value[:, 0:1024].astype(jnp.float32)
    return value[:, 0:1024] * jnp.exp2(value[:, 1024:1025])


def put(ref, k, value):
    for i in range(2):
        for j in range(8):
            ref[16 * k + 8 * i + j] = value[16 * i : 16 * i + 16, 128 * j : 128 * j + 128]


def take(ref, k):
    rows = [jnp.concatenate([ref[16 * k + 8 * i + j] for j in range(8)], axis=1) for i in range(2)]
    return jnp.concatenate(rows, axis=0)


def take_extra(ref, k):
    return jnp.concatenate([ref[16 * k], ref[16 * k + 1]], axis=0)


def put_extra(ref, k, value):
    ref[16 * k] = value[0:16]
    ref[16 * k + 1] = value[16:32]


def carry(send, value, *args):
    if value.dtype == jnp.bfloat16:
        return send(value, *args)
    return send(value.astype(jnp.float16), *args).astype(jnp.float32)


def merge(terms):
    terms = terms.astype(jnp.float32)
    return terms[0:8] + terms[8:16] + terms[16:24]


def places(pairs, slot):
    first, second = pairs[0, slot, 0], pairs[0, slot, 1]
    row, col = first // 8, second % 8
    dz, dx = (second // 8 // 4 - row // 4) & 3, (second // 8 % 4 - row % 4) & 3
    c = col % 2
    outer, inner = jnp.where(c == 0, dx, dz), jnp.where(c == 0, dz, dx)
    dy = (first % 8 // 2) ^ (col // 2)
    dy = dy ^ (dy >> 1)
    dy = jnp.where(first % 2 == 0, dy, (dy & 1) * 2 + (dy >> 1))
    return outer, inner, (first % 2) ^ c, dy


def load_right(pairs, slot, pair_gathered, rights):
    outer, inner, dc, dy = places(pairs, slot)
    for t in range(2):
        @pl.when(dc == t)
        def _():
            rights[...] = pair_gathered[t][dy]


def load_left(pairs, slot, gathered, lefts):
    outer, inner, dc, dy = places(pairs, slot)
    for t in range(4):
        @pl.when((-outer & 3) == t)
        def _():
            lefts[...] = take(gathered[t], -inner & 3)


def multiply(panel, matrix):
    return jnp.dot(panel[...], matrix, preferred_element_type=jnp.float32)


def store_mirror(pairs, slot, value, outs, half):
    outer, inner, dc, dy = places(pairs, slot)
    value = jnp.where(pairs[0, slot, 0] != pairs[0, slot, 1], value, 0.0)
    lanes = lax.broadcasted_iota(jnp.int32, (32, 128), 1)

    @pl.when(outer == 0)
    def _():
        outs[0][inner] = outs[0][inner] + value

    for t in range(1, 4):
        @pl.when(outer == t)
        def _():
            place = jnp.where(lanes == 8 * slot + inner, 1.0, 0.0)
            if half:
                coded = encode(value)
                put(outs[t], slot, coded[:, 0:1024])
                place = place + jnp.where(lanes == 8 * slot + 4, coded[:, 1024:1152], 0.0)
            else:
                put(outs[t], slot, value.astype(jnp.bfloat16))
            extra = take_extra(outs[t], 3).astype(jnp.float32) + place
            put_extra(outs[t], 3, extra.astype(outs[t].dtype))


def store_direct(pairs, slot, value, outs, results, half):
    outer, inner, dc, dy = places(pairs, slot)
    results[slot] = value
    results[3] = value

    def earlier(before, carry):
        @pl.when(pairs[0, before, 0] == pairs[0, slot, 0])
        def _():
            results[3] = results[3] + results[before]

        return carry

    lax.fori_loop(0, slot, earlier, 0)
    for t in range(2):
        @pl.when(dc == t)
        def _():
            if t and half:
                outs[1][dy] = encode(results[3])
            else:
                outs[t][dy, :, 0:1024] = results[3].astype(outs[t].dtype)


def add_gram(gathered, out, sent):
    gram = merge(take_extra(gathered[0], 4))
    for array in gathered[1:]:
        gram = gram + merge(take_extra(array, 4))
    out[...] = gram
    sent[0, :, 1024:1152] = split(gram)


def clear(outs):
    for out in outs:
        out[...] = jnp.zeros_like(out)


def mirror_kernel(half, pairs, live, blocks, h0, h1, *rest):
    outs, (rights,) = rest[:4], rest[4:]
    clear(outs)

    def advance(slot, carry):
        load_right(pairs, slot, (h0, h1), rights)
        store_mirror(pairs, slot, multiply(rights, blocks[slot]), outs, half)
        return carry

    lax.fori_loop(0, live[0], advance, 0)


def direct_kernel(half, pairs, live, turned, g0, g1, g2, g3, after, *rest):
    outs, (lefts, results) = rest[:-2], rest[-2:]
    clear(outs[:2])
    if not half:
        add_gram((g0, g1, g2, g3), outs[2], outs[1])

    def advance(slot, carry):
        load_left(pairs, slot, (g0, g1, g2, g3), lefts)
        store_direct(pairs, slot, multiply(lefts, turned[slot]), outs, results, half)
        return carry

    lax.fori_loop(0, live[0], advance, 0)


PANEL = pltpu.VMEM((32, 1024), jnp.bfloat16)
RESULTS = pltpu.VMEM((4, 32, 1024), jnp.float32)


def product_call(kernel, outs, scratch, name, pairs, live, *arrays):
    return pl.pallas_call(
        kernel,
        out_shape=outs,
        in_specs=[SMEM, SMEM] + [VMEM] * len(arrays),
        out_specs=[VMEM] * len(outs),
        scratch_shapes=scratch,
        compiler_params=PARAMS,
        name=name,
    )(pairs, live, *arrays)


def product(pairs, live, blocks, turned, gathered, pair_gathered, half):
    f32 = jnp.float32
    sent = f32 if half else jnp.bfloat16
    outs = [struct((4, 32, 1024), f32)] + [struct((50, 16, 128), sent)] * 3
    kernel = functools.partial(mirror_kernel, half)
    rows = product_call(kernel, outs, [PANEL], "mirror", pairs, live, blocks, *pair_gathered)
    outs = [struct((4, 32, 1024), f32), struct((4, 32, 1152), sent)]
    outs += [] if half else [struct((8, 128), f32)]
    kernel = functools.partial(direct_kernel, half)
    arrays = (turned, *gathered, rows[0])
    return rows + product_call(kernel, outs, [PANEL, RESULTS], "direct", pairs, live, *arrays)


def join_kernel(with_gram, *refs):
    parts, pair, joined, joined_pair = refs[:4], refs[4:6], refs[6], refs[7]
    for k, part in enumerate(parts):
        put(joined, k, part[:, 0:1024])
    if with_gram:
        gram = merge(parts[0][:, 1024:1152])
        for part in parts[1:]:
            gram = gram + merge(part[:, 1024:1152])
        put_extra(joined, 4, split(gram))
    else:
        put_extra(joined, 4, jnp.zeros((32, 128), jnp.bfloat16))
    for k, part in enumerate(pair):
        joined_pair[k] = part[...]


def join(parts, pair, with_gram):
    shapes = [(66, 16, 128), (2,) + pair[0].shape]
    return pl.pallas_call(
        functools.partial(join_kernel, with_gram),
        out_shape=[struct(shape, jnp.bfloat16) for shape in shapes],
        in_specs=[VMEM] * 6,
        out_specs=[VMEM] * 2,
        compiler_params=PARAMS,
        name="join",
    )(*parts, *pair)


def halve_kernel(with_gram, own, received, *rest):
    outs = rest[with_gram:]
    keep, send = outs[:2]
    half = keep.shape[0]
    for k in range(2 * half):
        value = own[k] + decode(received[k])
        if k < half:
            keep[k] = value
        elif not with_gram:
            send[k - half] = encode(value)
        else:
            send[k - half, :, 0:1024] = value.astype(send.dtype)
    if with_gram:
        gram = rest[0][...] + merge(received[0, :, 1024:1152])
        outs[2][...] = gram
        for k in range(half):
            send[k, :, 1024:1152] = split(gram)


def halve(own, received, gram):
    f32 = jnp.float32
    half = own.shape[0] // 2
    outs = [struct((half, 32, 1024), f32), struct((half,) + received.shape[1:], received.dtype)]
    outs += [struct((8, 128), f32)] * len(gram)
    return pl.pallas_call(
        functools.partial(halve_kernel, len(gram)),
        out_shape=outs,
        in_specs=[VMEM] * (2 + len(gram)),
        out_specs=[VMEM] * len(outs),
        compiler_params=PARAMS,
        name="halve",
    )(own, received, *gram)


def row_kernel(half, own, *refs):
    received, outs, (weights, total) = refs[:3], refs[3:7], refs[7:]
    entries = [(array, k) for array in received for k in range(3)]
    extras = [take_extra(array, 3).astype(jnp.float32) for array in received]
    powers = [jnp.exp2(extra) for extra in extras]
    for e, (array, k) in enumerate(entries):
        extra = extras[e // 3]
        scale = powers[e // 3][:, 8 * k + 4 : 8 * k + 5] if half else 1.0
        for s in range(4):
            weights[4 * e + s] = jnp.broadcast_to(extra[:, 8 * k + s : 8 * k + s + 1] * scale, (32, 128))
    for i in range(2):
        rows = slice(16 * i, 16 * i + 16)
        for j in range(8):
            columns = slice(128 * j, 128 * j + 128)
            sums = [own[s, rows, columns] for s in range(4)]
            for e, (array, k) in enumerate(entries):
                value = array[16 * k + 8 * i + j].astype(jnp.float32)
                for s in range(4):
                    sums[s] = sums[s] + value * weights[4 * e + s, rows]
            for s in range(4):
                total[s, rows, columns] = sums[s]
    outs[0][...] = total[0]
    for s in range(1, 4):
        outs[s][...] = encode(total[s]) if half else total[s].astype(outs[s].dtype)


def add_outer(own, received):
    half = received[0].dtype == jnp.float32
    sent = struct((32, 1152), jnp.float32) if half else struct((32, 1024), jnp.bfloat16)
    return pl.pallas_call(
        functools.partial(row_kernel, half),
        out_shape=[struct((32, 1024), jnp.float32)] + [sent] * 3,
        in_specs=[VMEM] * 4,
        out_specs=[VMEM] * 4,
        scratch_shapes=[pltpu.VMEM((36, 32, 128), jnp.float32), pltpu.VMEM((4, 32, 1024), jnp.float32)],
        compiler_params=PARAMS,
        name="add_outer",
    )(own, *received)


def add_parts(parts):
    value = parts[0][...] + parts[1][0]
    for part in parts[2:5]:
        value = value + decode(part[...])
    return value + decode(parts[5][0])


def first_kernel(*refs):
    parts, (first, panel, own) = refs[:6], refs[6:]
    value = add_parts(parts)
    first[...] = value
    rounded = value.astype(jnp.bfloat16)
    panel[:, 0:1024] = rounded
    own[...] = rounded
    panel[:, 1024:1152] = split(
        fold(
            lax.dot_general(
                rounded, rounded, (((1,), (1,)), ((), ())), preferred_element_type=jnp.float32
            )
        )
    )


def finish_first(parts):
    return pl.pallas_call(
        first_kernel,
        out_shape=[
            struct((32, 1024), jnp.float32),
            struct((32, 1152), jnp.bfloat16),
            struct((32, 1024), jnp.bfloat16),
        ],
        in_specs=[VMEM] * 6,
        out_specs=[VMEM] * 3,
        compiler_params=PARAMS,
        name="finish_first",
    )(*parts)


def second_kernel(*refs):
    parts, inverse, (scaled, gram) = refs[:6], refs[6], refs[7:]
    value = add_parts(parts)
    value = jnp.dot(inverse[...], value, precision=HIGHEST, preferred_element_type=jnp.float32)
    scaled[...] = value
    tile = fold(
        lax.dot_general(
            value, value, (((1,), (1,)), ((), ())), precision=HIGHEST, preferred_element_type=jnp.float32
        )
    )
    gram[...] = tile


def finish_second(parts, inverse):
    return pl.pallas_call(
        second_kernel,
        out_shape=[struct((32, 1024), jnp.float32), struct((8, 128), jnp.float32)],
        in_specs=[VMEM] * 7,
        out_specs=[VMEM] * 2,
        compiler_params=PARAMS,
        name="finish_second",
    )(*parts, inverse)


def total_kernel(own, other, out):
    total = own[...] + other[...]
    for k in range(64):
        out[k] = total


def total_gram(tile):
    tiles = pl.pallas_call(
        total_kernel,
        out_shape=struct((64, 8, 128), jnp.float32),
        in_specs=[VMEM] * 2,
        out_specs=VMEM,
        compiler_params=PARAMS,
        name="total_gram",
    )(tile, send_core(tile))
    return lax.all_to_all(tiles, ("z", "x", "y"), 0, 0, tiled=True)


def lower_inverse(gram):
    rows = lax.broadcasted_iota(jnp.int32, (32, 128), 0)
    lanes = lax.broadcasted_iota(jnp.int32, (32, 128), 1)
    wide = jnp.concatenate([gram, jnp.zeros((32, 96), jnp.float32)], axis=1)
    wide = jnp.where(lanes == rows + 32, 1.0, wide)
    parts = [wide[8 * k : 8 * k + 8] for k in range(4)]
    inside = rows[0:8]
    for step in range(4):
        columns = [
            [jnp.broadcast_to(part[:, k : k + 1], (8, 128)) for k in range(8 * step, 8 * step + 8)]
            for part in parts
        ]
        pivot = parts[step]
        schur = {(i, j): columns[step][j][i : i + 1] for i in range(8) for j in range(i + 1)}
        lines = [pivot[i : i + 1] for i in range(8)]
        factors, inverses = {}, []
        for j in range(8):
            inverses.append(1.0 / schur[j, j])
            for i in range(j + 1, 8):
                factors[i, j] = schur[i, j] * inverses[j]
            for i in range(j + 1, 8):
                for t in range(j + 1, i + 1):
                    schur[i, t] = schur[i, t] - factors[i, j] * schur[t, j]
                lines[i] = lines[i] - factors[i, j] * lines[j]
        for i in range(1, 8):
            pivot = jnp.where(inside == i, lines[i], pivot)
        parts[step] = pivot
        solved = [None] * 8
        for j in reversed(range(8)):
            value = lines[j] * inverses[j]
            for i in range(j + 1, 8):
                value = value - factors[i, j] * solved[i]
            solved[j] = value
        for later in range(step + 1, 4):
            for j in range(8):
                parts[later] = parts[later] - columns[later][j] * solved[j]
    wide = jnp.concatenate(parts, axis=0)
    diagonal = jnp.sum(jnp.where(lanes == rows, wide, 0.0), axis=1, keepdims=True)
    wide = wide / jnp.sqrt(diagonal)
    return wide[:, 32:64]


def factor_kernel(root, gram, panel, *outs):
    tile = gram[0]
    for k in range(1, 64):
        tile = tile + gram[k]
    inverse = lower_inverse(unfold(tile))
    outs[0][...] = (
        jnp.dot(inverse, panel[...], precision=HIGHEST, preferred_element_type=jnp.float32) * root
    )


def factor_first_kernel(root, gram, received, panel, basis, inverse):
    inverse[...] = lower_inverse(unfold(gram[...] + merge(received[0, :, 1024:1152])))
    basis[...] = (
        jnp.dot(inverse[...], panel[...], precision=HIGHEST, preferred_element_type=jnp.float32) * root
    )


def factor_first(gram, received, first, root):
    return pl.pallas_call(
        functools.partial(factor_first_kernel, root),
        out_shape=[struct((32, 1024), jnp.float32), struct((32, 32), jnp.float32)],
        in_specs=[VMEM] * 3,
        out_specs=[VMEM] * 2,
        compiler_params=PARAMS,
        cost_estimate=pl.CostEstimate(flops=1_000_000, bytes_accessed=10_000_000, transcendentals=0),
        name="factor_first",
    )(gram, received, first)


def factor_second(gram, scaled, root):
    return pl.pallas_call(
        functools.partial(factor_kernel, root),
        out_shape=struct((32, 1024), jnp.float32),
        in_specs=[VMEM] * 2,
        out_specs=VMEM,
        compiler_params=PARAMS,
        name="factor_second",
    )(gram, scaled)


SHIFTS = (1, 3, 2)


def spread(send, value):
    got = {s: send(value, s) for s in SHIFTS}
    return [value] + [got[s] for s in (1, 2, 3)]


def gather(panel, own, with_gram):
    inner, pair = join(spread(send_inner, panel), [own, send_y(own, 1)], with_gram)
    outer = spread(send_outer, inner)
    along_y = jnp.concatenate([pair, send_y(pair, 3)])
    return outer, [along_y, send_core(along_y)]


def scatter(parts):
    got = [carry(send_outer, parts[s], s) for s in (1, 2, 3)]
    column, send, *gram = halve(parts[4], carry(send_core, parts[5]), parts[6:])
    column, send, *gram = halve(column, carry(send_y, send, 3), gram)
    along_y = carry(send_y, send, 1)
    row = add_outer(parts[0], got)
    return [row[0], column] + [carry(send_inner, row[s], s) for s in (1, 2, 3)] + [along_y], gram


def turn_kernel(source, turned):
    for k in range(3):
        turned[k] = source[k].T


def turn(blocks):
    return pl.pallas_call(
        turn_kernel,
        out_shape=struct(blocks.shape, blocks.dtype),
        in_specs=[VMEM],
        out_specs=VMEM,
        compiler_params=PARAMS,
        cost_estimate=pl.CostEstimate(flops=0, bytes_accessed=6_000_000, transcendentals=0),
        name="turn",
    )(blocks)


def on_device(block_pairs, live_counts, pair_blocks, start_basis):
    users = 128 * start_basis.shape[2]
    root = float(users) ** 0.5
    turned = turn(pair_blocks)
    gathered, pair_gathered = gather(start_basis[0], start_basis[0], False)
    parts = product(block_pairs, live_counts, pair_blocks, turned, gathered, pair_gathered, True)
    first, panel, own = finish_first(scatter(parts)[0])
    gathered, pair_gathered = gather(panel, own, True)
    parts = product(block_pairs, live_counts, pair_blocks, turned, gathered, pair_gathered, False)
    parts, (gram,) = scatter(parts)
    first_basis, inverse = factor_first(gram, parts[5], first, root)
    scaled, tiles = finish_second(parts, inverse)
    embedding = factor_second(total_gram(tiles), scaled, root)
    return (first_basis[None], embedding[None])


def solution(mesh):
    mesh = Mesh(mesh.devices.reshape(4, 4, 4, 2), AXES)
    spec = P(AXES, None, None)
    return jax.shard_map(
        on_device, mesh=mesh, in_specs=(spec, P(AXES), spec, spec), out_specs=(spec, spec), check_vma=False
    )
```
